32 devices in a mesh: row: 4 (over y, x), col: 8 (over z, core).
Axes of the slice: x: 2, y: 2, z: 4, core: 2. Of those that a mesh axis runs over, the one named last changes fastest.
Arguments:
- fixed_section: bfloat16 [128, 1024], P('row', 'col'), may hold values from -6 to 6
- moving_section: bfloat16 [128, 1024], P('row', 'col'), may hold values from -6 to 6
- field_init: float32 [2, 128, 1024], P(None, 'row', 'col'), may hold values from -48 to 48
- first_weight: float32 [8, 9], replicated, may hold values from -2 to 2
- first_bias: float32 [8], replicated, may hold values from -0.5 to 0.5
- second_weight: float32 [8, 8, 9], replicated, may hold values from -0.75 to 0.75
Outputs:
- field_change: float32 [2, 128, 1024], P(None, 'row', 'col')
The draws below stay inside these ranges and needn't reach their ends.
All inputs are finite; a program needn't handle non-finite values.
Results may differ from the reference program's by a relative error of at most 0.011.
Values may be sent and summed in bfloat16 or wider, within the bound.
No kernel may reach another device: no remote copies, remote signals or barrier semaphores. Data moves between devices by JAX's collectives and lax.ppermute only.
A program may use at most 64 MiB of HBM per device.

```python
import jax
import jax.numpy as jnp
from jax import lax

CH = 8
REACH = 16
ITERS = 3
H = 128
W = 1024


def shard_levels(own_key, dims, pieces, least, high):
    def one(axis_at, parts):
        heights = jax.random.uniform(jax.random.fold_in(jax.random.fold_in(own_key, 6), axis_at), (parts,), jnp.float32, least / len(pieces), high / len(pieces))
        return jnp.repeat(jnp.exp(heights), dims[axis_at] // parts).reshape((-1,) + (1,) * (len(dims) - axis_at - 1))

    factor_of = one(*pieces[0])
    for cut in pieces[1:]:
        factor_of = factor_of * one(*cut)
    return factor_of


def scatter_about(stream_key, dims, width, most, pieces=(), held_as=jnp.bfloat16):
    drawn = jax.random.normal(stream_key, dims, jnp.float32) * width
    if len(pieces) > 0:
        drawn = shard_levels(stream_key, dims, pieces, -0.22, 0.18) * drawn
    return jnp.clip(drawn, min=-most, max=most).astype(held_as)


def setup_inputs(seed: int = 0) -> dict:
    seeds = jax.random.split(jax.random.key(seed), 7)
    return {
        "fixed_section": scatter_about(seeds[0], (H, W), 1.0, 6.0, ((0, 4), (1, 8))),
        "moving_section": scatter_about(seeds[1], (H, W), 1.0, 6.0, ((0, 4), (1, 8))),
        "field_init": scatter_about(seeds[2], (2, H, W), REACH, 48.0, ((1, 4), (2, 8)), jnp.float32),
        "first_weight": scatter_about(seeds[3], (CH, 9), 9 ** -0.5, 2.0, (), jnp.float32),
        "first_bias": jnp.clip(jax.random.uniform(seeds[4], (CH,), jnp.float32, -0.5, 0.5), -0.5, 0.5),
        "second_weight": scatter_about(seeds[5], (CH, CH, 9), (9 * CH) ** -0.5, 0.75, (), jnp.float32),
    }


stiffness = 0.01
step_size = 0.5
adam_epsilon = 0.01

def encode(image_ext, first_weight, first_bias, second_weight, first_mask):
    out_rows = image_ext.shape[0] - 2
    out_cols = image_ext.shape[1] - 2
    hidden = jnp.zeros((first_weight.shape[0], out_rows, out_cols), jnp.float32) + first_bias[:, None, None]
    for tap_index in range(9):
        tap_row = tap_index // 3
        tap_col = tap_index % 3
        hidden = hidden + first_weight[:, tap_index, None, None] * image_ext[None, tap_row:tap_row + out_rows, tap_col:tap_col + out_cols]
    hidden = jnp.maximum(hidden, 0.0) * first_mask
    out_rows = out_rows - 2
    out_cols = out_cols - 2
    embedding = jnp.zeros((second_weight.shape[0], out_rows, out_cols), jnp.float32)
    for tap_index in range(9):
        tap_row = tap_index // 3
        tap_col = tap_index % 3
        embedding = embedding + jnp.einsum('oc,chw->ohw', second_weight[:, :, tap_index], hidden[:, tap_row:tap_row + out_rows, tap_col:tap_col + out_cols], precision=lax.Precision.HIGHEST)
    return embedding

def sample(flattened, ext_cols, displace, margin, fixed_embedding):
    channels = fixed_embedding.shape[0]
    out_rows = displace.shape[1]
    out_cols = displace.shape[2]
    nearest = jnp.floor(displace + 0.5)
    fraction = displace - nearest
    offsets = nearest.astype(jnp.int32)
    spline = [0.5 * (0.5 - fraction) ** 2, 0.75 - fraction * fraction, 0.5 * (0.5 + fraction) ** 2]
    slopes = [fraction - 0.5, -2.0 * fraction, 0.5 + fraction]
    base_row = lax.broadcasted_iota(jnp.int32, (out_rows, out_cols), 0) + margin + offsets[0]
    base_col = lax.broadcasted_iota(jnp.int32, (out_rows, out_cols), 1) + margin + offsets[1]
    warped = jnp.zeros((channels, out_rows, out_cols), jnp.float32)
    along_row = jnp.zeros((channels, out_rows, out_cols), jnp.float32)
    along_col = jnp.zeros((channels, out_rows, out_cols), jnp.float32)
    for tap_row in range(3):
        for tap_col in range(3):
            position = (base_row + (tap_row - 1)) * ext_cols + base_col + (tap_col - 1)
            picked = jnp.take(flattened, position.reshape(-1), axis=1).reshape(channels, out_rows, out_cols)
            warped = warped + (spline[tap_row][0] * spline[tap_col][1])[None] * picked
            along_row = along_row + (slopes[tap_row][0] * spline[tap_col][1])[None] * picked
            along_col = along_col + (spline[tap_row][0] * slopes[tap_col][1])[None] * picked
    mismatch = warped - fixed_embedding
    factor = 2.0 / channels
    return jnp.stack([lax.optimization_barrier(jnp.sum(mismatch * along_row, axis=0)) * factor, lax.optimization_barrier(jnp.sum(mismatch * along_col, axis=0)) * factor])

def reference(fixed_section, moving_section, field_init, first_weight, first_bias, second_weight):
    full_rows, full_cols = fixed_section.shape
    margin = REACH + 1
    mask_rows = lax.broadcasted_iota(jnp.int32, (full_rows + 2, full_cols + 2), 0) - 1
    mask_cols = lax.broadcasted_iota(jnp.int32, (full_rows + 2, full_cols + 2), 1) - 1
    first_mask = ((mask_rows >= 0) & (mask_rows < full_rows) & (mask_cols >= 0) & (mask_cols < full_cols)).astype(jnp.float32)
    fixed_embedding = encode(jnp.pad(fixed_section.astype(jnp.float32), 2), first_weight, first_bias, second_weight, first_mask)
    moving_embedding = encode(jnp.pad(moving_section.astype(jnp.float32), 2), first_weight, first_bias, second_weight, first_mask)
    padded_moving = jnp.pad(moving_embedding, ((0, 0), (margin, margin), (margin, margin)))
    channels, ext_rows, ext_cols = padded_moving.shape
    flattened = padded_moving.reshape(channels, ext_rows * ext_cols)
    raw_field = field_init
    first_moment = jnp.zeros_like(field_init)
    second_moment = jnp.zeros_like(field_init)
    for iteration in range(ITERS):
        squashed = jnp.tanh(raw_field / REACH)
        displace = REACH * squashed
        data_term = sample(flattened, ext_cols, displace, margin, fixed_embedding)
        padded = jnp.pad(displace, ((0, 0), (1, 1), (1, 1)))
        neighbours = padded[:, 2:, 1:-1] + padded[:, :-2, 1:-1] + padded[:, 1:-1, 2:] + padded[:, 1:-1, :-2]
        gradient = (data_term + 2.0 * stiffness * (4.0 * displace - neighbours)) * (1.0 - squashed * squashed)
        first_moment = 0.9 * first_moment + 0.1 * gradient
        second_moment = 0.999 * second_moment + 0.001 * gradient * gradient
        corrected_one = first_moment / (1.0 - 0.9 ** (iteration + 1))
        corrected_two = second_moment / (1.0 - 0.999 ** (iteration + 1))
        raw_field = raw_field - step_size * corrected_one / (jnp.sqrt(corrected_two) + adam_epsilon)
    return raw_field - field_init
```

```python
import functools

import jax
import jax.numpy as jnp
import numpy as np
from jax import lax
from jax.experimental import pallas as pl
from jax.experimental.pallas import tpu as pltpu
from jax.sharding import PartitionSpec as P

CH = 8
REACH = 16
ITERS = 3
STIFFNESS = 0.01
STEP = 0.5
EPS = 0.01

TR, TC = 32, 128
HALF = 64
SIDE = 3
PITCH = HALF + 2 * SIDE
FROWS = TR + 2 * SIDE
NQ = 22
HALO_M = REACH + 1 + 2 + 2
HALO_F = 4
LANE0 = HALO_M
EROWS = 72
HROWS = 80
IROWS = 80
FE_BLOCKS = 5
ME_BLOCKS = 9


def _levels(span):
    out = []
    while span > 1:
        cut = (span + 1) // 2
        out.append(cut)
        span = cut
    return out


def _groups():
    out = []
    for g in range(NQ // 2):
        first = max((256 * g) // PITCH - SIDE, -2)
        last = min((256 * g + 255) // PITCH - SIDE, TR + 1)
        start = first + 2
        start -= start % 2
        span = last + 18 + REACH - start + 1
        out.append((start, span + 2, span))
    return out


GROUPS = _groups()


def _split(x):
    hi = x.astype(jnp.bfloat16)
    lo = (x - hi.astype(jnp.float32)).astype(jnp.bfloat16)
    return hi, lo


def _roll(x, shift, axis):
    size = x.shape[axis]
    shift = shift % size
    return x if shift == 0 else pltpu.roll(x, shift, axis)


def _dot(a, b):
    return jnp.dot(a, b, preferred_element_type=jnp.float32)


def _kernel(where_ref, mw_ref, fw_ref, fi_ref, b1_ref, bias_ref, w2_ref, out_ref,
            hs, e3, ef, raw, m1, m2, sq, disp, idx, dat):
    row0, col0 = where_ref[0], where_ref[1]
    rows, cols = where_ref[2], where_ref[3]
    lane = lax.broadcasted_iota(jnp.int32, (CH, 128), 1)
    col_ok = []
    for h in range(2):
        c = col0 + HALF * h - LANE0 + lane
        col_ok.append((c >= 0) & (c < cols))
    bias = jnp.broadcast_to(bias_ref[...], (CH, 128))

    def keep(y, h):
        r = row0 + y
        ok = jnp.where((r >= 0) & (r < rows), 1, 0)
        return jnp.where(col_ok[h], ok.astype(jnp.float32), 0.0)

    def embed(image_ref, top, blocks, sink):
        hidden = 8 * blocks + 2
        hidden += hidden % 2
        if hidden > 72:
            hidden = 72
        image = image_ref[...].astype(jnp.float32)
        parts = []
        for kx in range(3):
            parts.append(jnp.concatenate(
                [_roll(image[:, 128 * h:128 * h + 128], 1 - kx, 1) for h in range(2)], axis=1))
        stack = jnp.concatenate(parts, axis=0).astype(jnp.bfloat16)
        pre = _dot(b1_ref[0, :CH * hidden], stack) + _dot(b1_ref[1, :CH * hidden], stack)
        for p in range(0, hidden, 2):
            for h in range(2):
                pair = []
                for q in (p, p + 1):
                    v = pre[CH * q:CH * q + CH, 128 * h:128 * h + 128] + bias
                    pair.append(jnp.maximum(v, 0.0) * keep(top - 1 + q, h))
                v = jnp.concatenate(pair, axis=0)
                for kx in range(3):
                    hi, lo = _split(_roll(v, 1 - kx, 1))
                    hs[0, kx, CH * p:CH * p + 16, 128 * h:128 * h + 128] = hi
                    hs[1, kx, CH * p:CH * p + 16, 128 * h:128 * h + 128] = lo
        for p in range(hidden, 8 * blocks + 2, 2):
            for kx in range(3):
                for piece in range(2):
                    hs[piece, kx, CH * p:CH * p + 16, :] = jnp.zeros((16, 256), jnp.bfloat16)
        for b in range(blocks):
            hi = jnp.concatenate([hs[0, kx, 64 * b:64 * b + 80] for kx in range(3)], axis=0)
            lo = jnp.concatenate([hs[1, kx, 64 * b:64 * b + 80] for kx in range(3)], axis=0)
            t = _dot(w2_ref[...], hi)
            v = t[:64] + t[64:] + _dot(w2_ref[:64], lo)
            for h in range(2):
                got = []
                for k in range(8):
                    got.append(v[CH * k:CH * k + CH, 128 * h:128 * h + 128] * keep(top + 8 * b + k, h))
                sink(b, h, got)

    fixed_rows = [[], []]

    def fixed_sink(b, h, got):
        fixed_rows[h].extend(got)

    embed(fw_ref, -2, FE_BLOCKS, fixed_sink)
    for h in range(2):
        cur = jnp.zeros((CH, 128), jnp.float32)
        q = 0
        for i in range(36):
            f0 = PITCH * (i + 1)
            at, o = f0 // 128, f0 % 128
            while q < at:
                ef[h, q] = cur
                q += 1
            v = _roll(fixed_rows[h][i], o - (LANE0 - SIDE), 1)
            cur = jnp.where(lane >= o, v, cur)
            if o + PITCH > 128:
                ef[h, q] = cur
                q += 1
                cur = v
        while q < NQ:
            ef[h, q] = cur
            q += 1

    def moving_sink(b, h, got):
        out = []
        for e0 in got:
            left, right = _roll(e0, 1, 1), _roll(e0, -1, 1)
            p1 = 0.5 * (right - left)
            p2 = 0.5 * (right + left) - e0
            out += [e0 + 0.25 * p2, p1, p2]
        hi, lo = _split(jnp.concatenate(out, axis=0))
        e3[h, 192 * b:192 * b + 192, 0:128] = hi
        e3[h, 192 * b:192 * b + 192, 128:256] = lo

    embed(mw_ref, -(REACH + 3), ME_BLOCKS, moving_sink)

    cur = jnp.zeros((8, 128), jnp.float32)
    q = 0
    for i in range(FROWS):
        f0 = PITCH * i
        at, o = f0 // 128, f0 % 128
        v = _roll(fi_ref[i], o - (LANE0 - SIDE), 1)
        cur = jnp.where(lane >= o, v, cur)
        if o + PITCH > 128:
            raw[at] = cur
            cur = v
            q = at + 1
    while q < NQ:
        raw[q] = cur
        q += 1
    m1[...] = jnp.zeros_like(m1)
    m2[...] = jnp.zeros_like(m2)
    dat[...] = jnp.zeros_like(dat)

    sub = lax.broadcasted_iota(jnp.int32, (8, 128), 0)
    half_at = HALF * (sub % 2)

    def place(q):
        f = lax.broadcasted_iota(jnp.int32, (8, 128), 1) + 128 * q
        y = jnp.floor((f.astype(jnp.float32) + 0.5) * (1.0 / PITCH)).astype(jnp.int32)
        return y - SIDE, f - y * PITCH

    def shifted(x, q, s):
        if s > 0:
            a = _roll(x[q], -s, 1)
            b = _roll(x[min(q + 1, NQ - 1)], -s, 1)
            return jnp.where(lane < 128 - s, a, b)
        a = _roll(x[q], -s, 1)
        b = _roll(x[max(q - 1, 0)], -s, 1)
        return jnp.where(lane >= -s, a, b)

    iota_k = lax.broadcasted_iota(jnp.int32, (128, 256), 0).astype(jnp.float32).astype(jnp.bfloat16)

    def group(g, h):
        start, count, span = GROUPS[g]

        def pair(ref, s):
            return jnp.concatenate([jnp.broadcast_to(ref[2 * g + k, s:s + 1, :], (8, 128)) for k in range(2)], axis=1)

        col = jnp.concatenate([idx[2 * g + k, 2 + h:3 + h, :] for k in range(2)], axis=1).astype(jnp.bfloat16)
        pick = jnp.where(iota_k == jnp.broadcast_to(col, (128, 256)), jnp.bfloat16(1.0), jnp.bfloat16(0.0))
        t = _dot(e3[h, 24 * start:24 * (start + count), :], jnp.concatenate([pick, pick], axis=0))
        base = pair(idx, h) - (start * 1.0)
        conds = []
        for cut in _levels(span):
            c = base >= cut
            conds.append((cut, c))
            base = jnp.where(c, base - cut, base)
        taps = []
        for b in range(3):
            T = [t[24 * k + 8 * b:24 * k + 8 * b + 8] for k in range(count)]
            for cut, c in conds:
                T = [jnp.where(c, T[k + cut], T[k]) if k + cut < len(T) else T[k] for k in range(cut + 2)]
            taps.append(T)
        fr, fc = pair(disp, 4 + h), pair(disp, 6 + h)
        A, B = [], []
        for a in range(3):
            w = fc * taps[2][a]
            v = taps[1][a] + w
            A.append(taps[0][a] + fc * v)
            B.append(v + w)
        da, qa = 0.5 * (A[2] - A[0]), 0.5 * (A[2] + A[0]) - A[1]
        db, qb = 0.5 * (B[2] - B[0]), 0.5 * (B[2] + B[0]) - B[1]
        wa = fr * qa
        va = da + wa
        warped = A[1] + 0.25 * qa + fr * va
        slope_row = va + wa
        slope_col = B[1] + 0.25 * qb + fr * (db + fr * qb)
        fixed = jnp.concatenate([ef[h, 2 * g], ef[h, 2 * g + 1]], axis=1)
        miss = (warped - fixed) * (2.0 / CH)
        for comp, slope in ((0, slope_row), (1, slope_col)):
            total = jnp.sum(miss * slope, axis=0, keepdims=True)
            for k in range(2):
                s = 2 * comp + h
                dat[2 * g + k, s:s + 1, :] = total[:, 128 * k:128 * k + 128]

    def step(t, _):
        for q in range(NQ):
            y, j = place(q)
            c = col0 + half_at + j - SIDE
            ok = (row0 + y >= 0) & (row0 + y < rows) & (c >= 0) & (c < cols)
            s = jnp.tanh(raw[q] * (1.0 / REACH))
            d = REACH * s
            n = jnp.floor(d + 0.5)
            sq[q] = s
            fr = d - n
            disp[q] = jnp.where(sub < 4, jnp.where(ok, d, 0.0), _roll(fr, 4, 0))
            first = jnp.where(sub < 2, (y + 18).astype(jnp.float32), (j + (LANE0 - SIDE)).astype(jnp.float32))
            idx[q] = jnp.maximum(n + first, 0.0)
        for g in range(NQ // 2 - 1):
            for h in range(2):
                group(g, h)

        @pl.when(t == 0)
        def _():
            for h in range(2):
                group(NQ // 2 - 1, h)

        tf = (t + 1).astype(jnp.float32)
        one = jnp.where(t == 0, 1.0 / (1.0 - 0.9), jnp.where(t == 1, 1.0 / (1.0 - 0.9 ** 2), 1.0 / (1.0 - 0.9 ** 3)))
        two = jnp.where(t == 0, 1.0 / (1.0 - 0.999), jnp.where(t == 1, 1.0 / (1.0 - 0.999 ** 2), 1.0 / (1.0 - 0.999 ** 3)))
        for q in range(NQ):
            around = shifted(disp, q, 1) + shifted(disp, q, -1) + shifted(disp, q, PITCH) + shifted(disp, q, -PITCH)
            s = sq[q]
            grad = (dat[q] + 2.0 * STIFFNESS * (4.0 * REACH * s - around)) * (1.0 - s * s)
            a = 0.9 * m1[q] + 0.1 * grad
            b = 0.999 * m2[q] + 0.001 * grad * grad
            m1[q] = a
            m2[q] = b
            raw[q] = raw[q] - STEP * (a * one) / (jnp.sqrt(b * two) + EPS)
        return 0

    lax.fori_loop(0, ITERS, step, 0)

    for y in range(TR):
        f0 = PITCH * (y + SIDE) + SIDE
        at, o = f0 // 128, f0 % 128
        v = raw[at]
        if o + HALF > 128:
            v = jnp.where(lane >= o, v, raw[at + 1])
        v = _roll(v, -o, 1) - _roll(fi_ref[y + SIDE], -LANE0, 1)
        w = _roll(v, HALF, 1)
        for comp in range(2):
            out_ref[comp, y:y + 1, 0:HALF] = v[2 * comp:2 * comp + 1, 0:HALF]
            out_ref[comp, y:y + 1, HALF:TC] = w[2 * comp + 1:2 * comp + 2, HALF:TC]


def _swaps(n, first):
    out = []
    for a in range(first, n - 1, 2):
        out += [(a, a + 1), (a + 1, a)]
    return out


def _exchange(low, high, axis):
    n = lax.axis_size(axis)
    even = lax.axis_index(axis) % 2 == 0
    one = lax.ppermute(jnp.where(even, high, low), axis, _swaps(n, 0))
    two = lax.ppermute(jnp.where(even, low, high), axis, _swaps(n, 1))
    return jnp.where(even, two, one), jnp.where(even, one, two)


def _pieces(x):
    hi = lax.reduce_precision(x, 8, 7)
    return hi.astype(jnp.bfloat16), (x - hi).astype(jnp.bfloat16)


def _toeplitz(first_weight, second_weight):
    w1 = first_weight.reshape(CH, 3, 3)
    p = np.arange(72)[:, None, None, None]
    i = np.arange(IROWS)[None, None, None, :]
    b1 = sum(jnp.where(i - p == ky, w1[None, :, ky, :, None], 0.0) for ky in range(3))
    b1 = b1.reshape(72 * CH, 3 * IROWS)
    w2 = second_weight.reshape(CH, CH, 3, 3).transpose(0, 3, 2, 1)
    yy = np.arange(8)[:, None, None, None, None]
    yp = np.arange(10)[None, None, None, :, None]
    b2 = sum(jnp.where(yp - yy == ky, w2[None, :, :, ky, None, :], 0.0) for ky in range(3))
    b2 = b2.reshape(8 * CH, 3 * 10 * CH)
    return jnp.stack(_pieces(b1)), jnp.concatenate(_pieces(b2), axis=0)


def _local(fixed_section, moving_section, field_init, first_weight, first_bias, second_weight):
    row0 = lax.axis_index("row") * TR
    col0 = lax.axis_index("col") * TC
    where = jnp.stack([row0, col0, TR * lax.axis_size("row"), TC * lax.axis_size("col")]).astype(jnp.int32)
    b1, w2 = _toeplitz(first_weight, second_weight)

    parts = [moving_section.astype(jnp.float32), fixed_section.astype(jnp.float32), field_init[0], field_init[1]]
    halos = [HALO_M, HALO_F, SIDE, SIDE]
    low = jnp.concatenate([x[:n] for x, n in zip(parts, halos)], axis=0)
    high = jnp.concatenate([x[TR - n:] for x, n in zip(parts, halos)], axis=0)
    below, above = _exchange(low, high, "row")
    tall, at = [], 0
    for x, n in zip(parts, halos):
        tall.append(jnp.concatenate([below[at:at + n], x, above[at:at + n]], axis=0))
        at += n
    full = TR + 2 * HALO_M

    def pad(x):
        return jnp.pad(x, ((0, full - x.shape[0]), (0, 0)))

    low = jnp.concatenate([pad(x[:, :n]) for x, n in zip(tall, halos)], axis=1)
    high = jnp.concatenate([pad(x[:, TC - n:]) for x, n in zip(tall, halos)], axis=1)
    left, right = _exchange(low, high, "col")
    wide, at = [], 0
    for x, n in zip(tall, halos):
        r = x.shape[0]
        x = jnp.concatenate([left[:r, at:at + n], x, right[:r, at:at + n]], axis=1)
        x = jnp.pad(x, ((0, 0), (LANE0 - n, HALF + TC - LANE0 - TC - n)))
        wide.append(jnp.concatenate([x[:, :128], x[:, HALF:HALF + 128]], axis=1))
        at += n
    mw, fw = [jnp.pad(x, ((0, IROWS - x.shape[0]), (0, 0))).astype(jnp.bfloat16) for x in wide[:2]]
    fi = jnp.stack([wide[2][:, :128], wide[2][:, 128:], wide[3][:, :128], wide[3][:, 128:]], axis=1)
    fi = jnp.pad(fi, ((0, 0), (0, 4), (0, 0)))

    vmem = pl.BlockSpec(memory_space=pltpu.VMEM)
    f32 = jnp.float32
    return pl.pallas_call(
        _kernel,
        out_shape=jax.ShapeDtypeStruct((2, TR, TC), f32),
        in_specs=[pl.BlockSpec(memory_space=pltpu.SMEM)] + [vmem] * 6,
        out_specs=vmem,
        scratch_shapes=[
            pltpu.VMEM((2, 3, HROWS * CH, 256), jnp.bfloat16),
            pltpu.VMEM((2, EROWS * 24, 256), jnp.bfloat16),
            pltpu.VMEM((2, NQ, CH, 128), f32),
            *[pltpu.VMEM((NQ, 8, 128), f32) for _ in range(7)],
        ],
        compiler_params=pltpu.CompilerParams(vmem_limit_bytes=48 * 2 ** 20),
    )(where, mw, fw, fi, b1, first_bias[:, None], w2)


def solution(mesh):
    return jax.shard_map(
        _local,
        mesh=mesh,
        in_specs=(P("row", "col"), P("row", "col"), P(None, "row", "col"), P(), P(), P()),
        out_specs=P(None, "row", "col"),
        check_vma=False,
    )
```

```python
import jax
import jax.numpy as jnp
from jax import lax
from jax.experimental import pallas as pl
from jax.experimental.pallas import tpu as pltpu
from jax.sharding import PartitionSpec as P

CH = 8
REACH = 16
ITERS = 3
STIFFNESS = 0.01
STEP = 0.5
EPS = 0.01

TR, TC = 32, 128
HALF = 64
SIDE = 3
PITCH = HALF + 2 * SIDE
FROWS = TR + 2 * SIDE
NQ = 22
HALO_M = REACH + 1 + 2 + 2
LANE0 = HALO_M
EROWS = 72
HROWS = 80
HALO_PAD = 24
PADS = (HALO_PAD, 8, 8, 8)
TALL = TR + 2 * HALO_PAD
FE_BLOCKS = 5
ME_BLOCKS = 9


def _levels(span):
    out = []
    while span > 1:
        cut = (span + 1) // 2
        out.append(cut)
        span = cut
    return out


def _groups():
    out = []
    for g in range(NQ // 2):
        first = max((256 * g) // PITCH - SIDE, -2)
        last = min((256 * g + 255) // PITCH - SIDE, TR + 1)
        start = first + 2
        start -= start % 2
        span = last + 18 + REACH - start + 1
        out.append((start, span + 2, span))
    return out


GROUPS = _groups()


def _split(x):
    hi = x.astype(jnp.bfloat16)
    lo = (x - hi.astype(jnp.float32)).astype(jnp.bfloat16)
    return hi, lo


def _roll(x, shift, axis):
    size = x.shape[axis]
    shift = shift % size
    return x if shift == 0 else pltpu.roll(x, shift, axis)


def _pick(x, index):
    dims = lax.GatherDimensionNumbers(
        offset_dims=(), collapsed_slice_dims=(1,), start_index_map=(1,),
        operand_batching_dims=(0,), start_indices_batching_dims=(0,))
    return lax.gather(x, index[..., None], dims, (1, 1), mode=lax.GatherScatterMode.PROMISE_IN_BOUNDS)


def _dot(a, b):
    return jnp.dot(a, b, preferred_element_type=jnp.float32)


def _tall(own, one, two):
    r, n = lax.axis_index("row"), lax.axis_size("row")
    even = lax.rem(r, 2) == 0
    above = jnp.where(r > 0, jnp.where(even, two, one), 0.0)
    below = jnp.where(r < n - 1, jnp.where(even, one, two), 0.0)
    out, at = [], 0
    for x, pad in zip(own, PADS):
        out.append(jnp.concatenate([above[at:at + pad], x, below[at:at + pad]], axis=0))
        at += pad
    return out


def _fetch(pairs, sems):
    copies = [pltpu.make_async_copy(src, dst, sems.at[k]) for k, (src, dst) in enumerate(pairs)]
    for copy in copies:
        copy.start()
    for copy in copies:
        copy.wait()


def _own(own_ref):
    return [own_ref[TR * k:TR * k + TR] for k in range(4)]


def _pack_rows(mv_ref, fx_ref, fd_ref, one_ref, two_ref, own_ref, mv, fx, fd, sems):
    _fetch([(mv_ref, mv), (fx_ref, fx), (fd_ref, fd)], sems)
    even = lax.rem(lax.axis_index("row"), 2) == 0
    at = 0
    for k, x in enumerate([mv[...].astype(jnp.float32), fx[...].astype(jnp.float32), fd[0], fd[1]]):
        pad = PADS[k]
        own_ref[TR * k:TR * k + TR] = x
        first, last = x[:pad], x[TR - pad:]
        one_ref[at:at + pad] = jnp.where(even, last, first)
        two_ref[at:at + pad] = jnp.where(even, first, last)
        at += pad


def _weights(w1_ref, w2_ref, bias_ref, m1_ref, m2_ref, b_ref, w1, w2, flat, sems):
    _fetch([(w1_ref, w1), (w2_ref, w2)], sems)
    lane = lax.broadcasted_iota(jnp.int32, (CH, 128), 1)
    sub = lax.broadcasted_iota(jnp.int32, (CH, 128), 0)
    flat[0] = jnp.zeros((CH, 128), jnp.float32)
    flat[1] = jnp.zeros((CH, 128), jnp.float32)
    flat[0, :, 0:9] = w1[...]
    for c2 in range(CH):
        flat[1, :, 9 * c2:9 * c2 + 9] = w2[:, c2, :]
    b = jnp.zeros((CH, 128), jnp.float32)
    for c in range(CH):
        b = jnp.where(sub == c, bias_ref[c], b)
    b_ref[...] = b
    hi_rows, lo_rows = [], []
    for y in range(8):
        ky = lane % 16 - y - (HALO_PAD - HALO_M)
        v = _pick(flat[0], jnp.clip(3 * ky + lane // 16, 0, 127))
        v = jnp.where((ky >= 0) & (ky <= 2), v, 0.0)
        hi = v.astype(jnp.bfloat16).astype(jnp.float32)
        hi_rows.append(hi)
        lo_rows.append(v - hi)
    m1_ref[...] = jnp.concatenate(hi_rows + lo_rows, axis=0)[:, :48].astype(jnp.bfloat16)
    hi_rows, lo_rows = [], []
    for kx in range(3):
        for y in range(8):
            halves = []
            for half in range(2):
                at = lane + 128 * half
                at = jnp.where(at >= 80, at - 80, at)
                ky = at // 8 - y
                v = _pick(flat[1], jnp.clip(9 * (at % 8) + 3 * ky + kx, 0, 127))
                halves.append(jnp.where((ky >= 0) & (ky <= 2), v, 0.0))
            v = jnp.concatenate(halves, axis=1)
            hi = v.astype(jnp.bfloat16).astype(jnp.float32)
            wide = lax.broadcasted_iota(jnp.int32, (CH, 256), 1)
            hi_rows.append(hi)
            lo_rows.append(jnp.where(wide < 80, v - hi, 0.0))
    m2_ref[...] = jnp.concatenate(hi_rows + lo_rows, axis=0)[:, :160].astype(jnp.bfloat16)


def _pack_cols(own_ref, up_ref, down_ref, one_ref, two_ref):
    even = lax.rem(lax.axis_index("col"), 2) == 0
    tall = _tall(_own(own_ref), up_ref[...], down_ref[...])
    lane = lax.broadcasted_iota(jnp.int32, (8, 128), 1)
    for i in range(TALL // 8):
        first = last = None
        for k in (3, 2, 1, 0):
            if 8 * i < tall[k].shape[0]:
                v = tall[k][8 * i:8 * i + 8]
                a, b = _roll(v, 32 * k, 1), _roll(v, 32 * k + HALO_M, 1)
                first = a if first is None else jnp.where(lane < 32 * k + 32, a, first)
                last = b if last is None else jnp.where(lane < 32 * k + 32, b, last)
        one_ref[8 * i:8 * i + 8] = jnp.where(even, last, first)
        two_ref[8 * i:8 * i + 8] = jnp.where(even, first, last)


def _windows(own, up, down, one, two):
    c, n = lax.axis_index("col"), lax.axis_size("col")
    even = lax.rem(c, 2) == 0
    left = jnp.where(c > 0, jnp.where(even, two, one), 0.0)
    right = jnp.where(c < n - 1, jnp.where(even, one, two), 0.0)
    out = []
    end = HALO_M - HALF + TC
    for k, x in enumerate(_tall(own, up, down)):
        lane = lax.broadcasted_iota(jnp.int32, x.shape, 1)
        r = x.shape[0]
        lw = jnp.where(lane < HALO_M, _roll(left[:r], -32 * k, 1), _roll(x, HALO_M, 1))
        rw = jnp.where(lane < end, _roll(x, HALO_M - HALF, 1), _roll(right[:r], end - 32 * k, 1))
        out.append((lw, rw))
    return out


def _kernel(own_ref, up_ref, down_ref, one_ref, two_ref, w1_ref, bias_ref, w2_ref, out_ref,
            hs, e3, ef, raw, m1, m2, sq, disp, idx, dat):
    row0, col0 = TR * lax.axis_index("row"), TC * lax.axis_index("col")
    rows, cols = TR * lax.axis_size("row"), TC * lax.axis_size("col")
    lane = lax.broadcasted_iota(jnp.int32, (CH, 128), 1)
    col_ok = []
    for h in range(2):
        c = col0 + HALF * h - LANE0 + lane
        col_ok.append((c >= 0) & (c < cols))
    bias = bias_ref[...]
    moving, fixed, field0, field1 = _windows(
        _own(own_ref), up_ref[...], down_ref[...], one_ref[...], two_ref[...])
    field = [field0[0], field0[1], field1[0], field1[1]]

    def field_row(i):
        return jnp.concatenate([x[i + 8 - SIDE:i + 9 - SIDE] for x in field] + [jnp.zeros((4, 128), jnp.float32)], axis=0)

    def keep(y, h):
        r = row0 + y
        ok = jnp.where((r >= 0) & (r < rows), 1, 0)
        return jnp.where(col_ok[h], ok.astype(jnp.float32), 0.0)

    def embed(image, top, blocks, sink):
        shifted = [jnp.concatenate([_roll(image[h], 1 - kx, 1) for h in range(2)], axis=1) for kx in range(3)]
        known = image[0].shape[0]
        for b in range(blocks + 1):
            if 8 * b + 16 > known:
                for k in range(8 * b, 8 * blocks + 2, 2):
                    hs[0, CH * k:CH * k + 16] = jnp.zeros((16, 256), jnp.bfloat16)
                    hs[1, CH * k:CH * k + 16] = jnp.zeros((16, 256), jnp.bfloat16)
                break
            t = _dot(w1_ref[...], jnp.concatenate([x[8 * b:8 * b + 16] for x in shifted], axis=0).astype(jnp.bfloat16))
            pre = t[:64] + t[64:]
            for h in range(2):
                v = jnp.concatenate([
                    jnp.maximum(pre[CH * k:CH * k + CH, 128 * h:128 * h + 128] + bias, 0.0) * keep(top - 1 + 8 * b + k, h)
                    for k in range(8)], axis=0)
                hi, lo = _split(v)
                hs[0, 64 * b:64 * b + 64, 128 * h:128 * h + 128] = hi
                hs[1, 64 * b:64 * b + 64, 128 * h:128 * h + 128] = lo
        for b in range(blocks):
            t = _dot(w2_ref[...], jnp.concatenate([hs[0, 64 * b:64 * b + 80], hs[1, 64 * b:64 * b + 80]], axis=0))
            v = t[:192] + t[192:]
            for h in range(2):
                o = [v[64 * kx:64 * kx + 64, 128 * h:128 * h + 128] for kx in range(3)]
                e = o[1] + _roll(o[0], 1, 1) + _roll(o[2], -1, 1)
                sink(b, h, [e[CH * k:CH * k + CH] * keep(top + 8 * b + k, h) for k in range(8)])

    fixed_rows = [[], []]

    def fixed_sink(b, h, got):
        fixed_rows[h].extend(got)

    embed(fixed, -3, FE_BLOCKS, fixed_sink)
    for h in range(2):
        cur = jnp.zeros((CH, 128), jnp.float32)
        q = 0
        for i in range(36):
            f0 = PITCH * (i + 1)
            at, o = f0 // 128, f0 % 128
            while q < at:
                ef[h, q] = cur
                q += 1
            v = _roll(fixed_rows[h][i + 1], o - (LANE0 - SIDE), 1)
            cur = jnp.where(lane >= o, v, cur)
            if o + PITCH > 128:
                ef[h, q] = cur
                q += 1
                cur = v
        while q < NQ:
            ef[h, q] = cur
            q += 1

    def moving_sink(b, h, got):
        out = []
        for e0 in got:
            left, right = _roll(e0, 1, 1), _roll(e0, -1, 1)
            p1 = 0.5 * (right - left)
            p2 = 0.5 * (right + left) - e0
            out += [e0 + 0.25 * p2, p1, p2]
        hi, lo = _split(jnp.concatenate(out, axis=0))
        e3[h, 192 * b:192 * b + 192, 0:128] = hi
        e3[h, 192 * b:192 * b + 192, 128:256] = lo

    embed(moving, -(REACH + 3), ME_BLOCKS, moving_sink)

    cur = jnp.zeros((8, 128), jnp.float32)
    q = 0
    for i in range(FROWS):
        f0 = PITCH * i
        at, o = f0 // 128, f0 % 128
        v = _roll(field_row(i), o - (LANE0 - SIDE), 1)
        cur = jnp.where(lane >= o, v, cur)
        if o + PITCH > 128:
            raw[at] = cur
            cur = v
            q = at + 1
    while q < NQ:
        raw[q] = cur
        q += 1
    m1[...] = jnp.zeros_like(m1)
    m2[...] = jnp.zeros_like(m2)
    dat[...] = jnp.zeros_like(dat)

    sub = lax.broadcasted_iota(jnp.int32, (8, 128), 0)
    half_at = HALF * (sub % 2)

    def place(q):
        f = lax.broadcasted_iota(jnp.int32, (8, 128), 1) + 128 * q
        y = jnp.floor((f.astype(jnp.float32) + 0.5) * (1.0 / PITCH)).astype(jnp.int32)
        return y - SIDE, f - y * PITCH

    def shifted(x, q, s):
        if s > 0:
            a = _roll(x[q], -s, 1)
            b = _roll(x[min(q + 1, NQ - 1)], -s, 1)
            return jnp.where(lane < 128 - s, a, b)
        a = _roll(x[q], -s, 1)
        b = _roll(x[max(q - 1, 0)], -s, 1)
        return jnp.where(lane >= -s, a, b)

    iota_k = lax.broadcasted_iota(jnp.int32, (128, 256), 0).astype(jnp.float32).astype(jnp.bfloat16)

    def group(g, h):
        start, count, span = GROUPS[g]

        def pair(ref, s):
            return jnp.concatenate([jnp.broadcast_to(ref[2 * g + k, s:s + 1, :], (8, 128)) for k in range(2)], axis=1)

        col = jnp.concatenate([idx[2 * g + k, 2 + h:3 + h, :] for k in range(2)], axis=1).astype(jnp.bfloat16)
        pick = jnp.where(iota_k == jnp.broadcast_to(col, (128, 256)), jnp.bfloat16(1.0), jnp.bfloat16(0.0))
        t = _dot(e3[h, 24 * start:24 * (start + count), :], jnp.concatenate([pick, pick], axis=0))
        base = pair(idx, h) - (start * 1.0)
        conds = []
        for cut in _levels(span):
            c = base >= cut
            conds.append((cut, c))
            base = jnp.where(c, base - cut, base)
        taps = []
        for b in range(3):
            T = [t[24 * k + 8 * b:24 * k + 8 * b + 8] for k in range(count)]
            for cut, c in conds:
                T = [jnp.where(c, T[k + cut], T[k]) if k + cut < len(T) else T[k] for k in range(cut + 2)]
            taps.append(T)
        fr, fc = pair(disp, 4 + h), pair(disp, 6 + h)
        A, B = [], []
        for a in range(3):
            w = fc * taps[2][a]
            v = taps[1][a] + w
            A.append(taps[0][a] + fc * v)
            B.append(v + w)
        da, qa = 0.5 * (A[2] - A[0]), 0.5 * (A[2] + A[0]) - A[1]
        db, qb = 0.5 * (B[2] - B[0]), 0.5 * (B[2] + B[0]) - B[1]
        wa = fr * qa
        va = da + wa
        warped = A[1] + 0.25 * qa + fr * va
        slope_row = va + wa
        slope_col = B[1] + 0.25 * qb + fr * (db + fr * qb)
        fixed = jnp.concatenate([ef[h, 2 * g], ef[h, 2 * g + 1]], axis=1)
        miss = (warped - fixed) * (2.0 / CH)
        for comp, slope in ((0, slope_row), (1, slope_col)):
            total = jnp.sum(miss * slope, axis=0, keepdims=True)
            for k in range(2):
                s = 2 * comp + h
                dat[2 * g + k, s:s + 1, :] = total[:, 128 * k:128 * k + 128]

    def step(t):
        for q in range(NQ):
            y, j = place(q)
            c = col0 + half_at + j - SIDE
            ok = (row0 + y >= 0) & (row0 + y < rows) & (c >= 0) & (c < cols)
            s = jnp.tanh(raw[q] * (1.0 / REACH))
            d = REACH * s
            n = jnp.floor(d + 0.5)
            sq[q] = s
            fr = d - n
            disp[q] = jnp.where(sub < 4, jnp.where(ok, d, 0.0), _roll(fr, 4, 0))
            first = jnp.where(sub < 2, (y + 18).astype(jnp.float32), (j + (LANE0 - SIDE)).astype(jnp.float32))
            idx[q] = jnp.maximum(n + first, 0.0)
        for g in range(NQ // 2 - (t > 0)):
            for h in range(2):
                group(g, h)
        one, two = 1.0 / (1.0 - 0.9 ** (t + 1)), 1.0 / (1.0 - 0.999 ** (t + 1))
        for q in range(NQ):
            around = shifted(disp, q, 1) + shifted(disp, q, -1) + shifted(disp, q, PITCH) + shifted(disp, q, -PITCH)
            s = sq[q]
            grad = (dat[q] + 2.0 * STIFFNESS * (4.0 * REACH * s - around)) * (1.0 - s * s)
            a = 0.9 * m1[q] + 0.1 * grad
            b = 0.999 * m2[q] + 0.001 * grad * grad
            m1[q] = a
            m2[q] = b
            raw[q] = raw[q] - STEP * (a * one) / (jnp.sqrt(b * two) + EPS)

    for t in range(ITERS):
        step(t)

    for y in range(TR):
        f0 = PITCH * (y + SIDE) + SIDE
        at, o = f0 // 128, f0 % 128
        v = raw[at]
        if o + HALF > 128:
            v = jnp.where(lane >= o, v, raw[at + 1])
        v = _roll(v, -o, 1) - _roll(field_row(y + SIDE), -LANE0, 1)
        w = _roll(v, HALF, 1)
        for comp in range(2):
            out_ref[comp, y:y + 1, 0:HALF] = v[2 * comp:2 * comp + 1, 0:HALF]
            out_ref[comp, y:y + 1, HALF:TC] = w[2 * comp + 1:2 * comp + 2, HALF:TC]


def _swaps(n, first):
    return [p for a in range(first, n, 2) for p in ((a, (a + 1) % n), ((a + 1) % n, a))]


def _exchange(pair, axis):
    n = lax.axis_size(axis)
    return [lax.ppermute(x, axis, _swaps(n, k)) for k, x in enumerate(pair)]


def _local(fixed_section, moving_section, field_init, first_weight, first_bias, second_weight):
    vmem = pl.BlockSpec(memory_space=pltpu.VMEM)
    smem = pl.BlockSpec(memory_space=pltpu.SMEM)
    anywhere = pl.BlockSpec(memory_space=pltpu.HBM)
    f32, bf16 = jnp.float32, jnp.bfloat16

    def call(body, name, out, specs, scratch):
        return pl.pallas_call(
            body,
            out_shape=[jax.ShapeDtypeStruct(*x) for x in out],
            in_specs=specs,
            out_specs=[vmem] * len(out),
            scratch_shapes=scratch,
            compiler_params=pltpu.CompilerParams(vmem_limit_bytes=48 * 2 ** 20),
            name=name,
        )

    strip = ((sum(PADS), 128), f32)
    one, two, own = call(_pack_rows, "pack_rows", [strip, strip, ((4 * TR, TC), f32)], [anywhere] * 3, [
        pltpu.VMEM((TR, TC), bf16), pltpu.VMEM((TR, TC), bf16), pltpu.VMEM((2, TR, TC), f32),
        pltpu.SemaphoreType.DMA((3,))])(*[pltpu.with_memory_space_constraint(x, pltpu.HBM) for x in (moving_section, fixed_section, field_init)])
    up, down = _exchange((one, two), "row")
    w1, w2, bias = call(_weights, "weights", [((128, 48), bf16), ((384, 160), bf16), ((CH, 128), f32)],
                        [anywhere, anywhere, smem], [
        pltpu.VMEM((CH, 9), f32), pltpu.VMEM((CH, CH, 9), f32), pltpu.VMEM((2, CH, 128), f32),
        pltpu.SemaphoreType.DMA((2,))])(first_weight, second_weight, first_bias)
    strip = ((TALL, 128), f32)
    one, two = _exchange(call(_pack_cols, "pack_cols", [strip, strip], [vmem] * 3, [])(own, up, down), "col")
    return call(_kernel, "refine", [((2, TR, TC), f32)], [vmem] * 8, [
        pltpu.VMEM((2, HROWS * CH, 256), bf16),
        pltpu.VMEM((2, EROWS * 24, 256), bf16),
        pltpu.VMEM((2, NQ, CH, 128), f32),
        *[pltpu.VMEM((NQ, 8, 128), f32) for _ in range(7)],
    ])(own, up, down, one, two, w1, bias, w2)[0]


def solution(mesh):
    return jax.shard_map(
        _local,
        mesh=mesh,
        in_specs=(P("row", "col"), P("row", "col"), P(None, "row", "col"), P(), P(), P()),
        out_specs=P(None, "row", "col"),
        check_vma=False,
    )
```

```python
import jax
import jax.numpy as jnp
from jax import lax
from jax.experimental import pallas as pl
from jax.experimental.pallas import tpu as pltpu
from jax.sharding import PartitionSpec as P

CH = 8
REACH = 16
ITERS = 3
STIFFNESS = 0.01
STEP = 0.5
EPS = 0.01

TR, TC = 32, 128
HALF = 64
SIDE = 3
HALO_M = REACH + 1 + 2 + 2
HALO_PAD = 24
PADS = (HALO_PAD, 8, 8, 8)
TALL = TR + 2 * HALO_PAD
LANE0 = HALO_M
EROWS = 72
HROWS = 80
FE_BLOCKS = 5
ME_BLOCKS = 9

SEGS = 5
WIDE = 26
NQ = 10
CUT = 20
PROWS = EROWS - CUT


def _segment(s):
    return (0, -LANE0) if s < 3 else (1, HALF - LANE0)


def _levels(span):
    out = []
    while span > 1:
        cut = (span + 1) // 2
        out.append(cut)
        span = cut
    return out


def _split(x):
    hi = x.astype(jnp.bfloat16)
    lo = (x - hi.astype(jnp.float32)).astype(jnp.bfloat16)
    return hi, lo


def _roll(x, shift, axis):
    size = x.shape[axis]
    shift = shift % size
    return x if shift == 0 else pltpu.roll(x, shift, axis)


def _pick(x, index):
    dims = lax.GatherDimensionNumbers(
        offset_dims=(), collapsed_slice_dims=(1,), start_index_map=(1,),
        operand_batching_dims=(0,), start_indices_batching_dims=(0,))
    return lax.gather(x, index[..., None], dims, (1, 1), mode=lax.GatherScatterMode.PROMISE_IN_BOUNDS)


def _dot(a, b):
    return jnp.dot(a, b, preferred_element_type=jnp.float32)


def _tall(own, one, two):
    r, n = lax.axis_index("row"), lax.axis_size("row")
    even = lax.rem(r, 2) == 0
    above = jnp.where(r > 0, jnp.where(even, two, one), 0.0)
    below = jnp.where(r < n - 1, jnp.where(even, one, two), 0.0)
    out, at = [], 0
    for x, pad in zip(own, PADS):
        out.append(jnp.concatenate([above[at:at + pad], x, below[at:at + pad]], axis=0))
        at += pad
    return out


def _fetch(pairs, sems):
    copies = [pltpu.make_async_copy(src, dst, sems.at[k]) for k, (src, dst) in enumerate(pairs)]
    for copy in copies:
        copy.start()
    for copy in copies:
        copy.wait()


def _own(own_ref):
    return [own_ref[TR * k:TR * k + TR] for k in range(4)]


def _pack_rows(mv_ref, fx_ref, fd_ref, one_ref, two_ref, own_ref, mv, fx, fd, sems):
    _fetch([(mv_ref, mv), (fx_ref, fx), (fd_ref, fd)], sems)
    even = lax.rem(lax.axis_index("row"), 2) == 0
    at = 0
    for k, x in enumerate([mv[...].astype(jnp.float32), fx[...].astype(jnp.float32), fd[0], fd[1]]):
        pad = PADS[k]
        own_ref[TR * k:TR * k + TR] = x
        first, last = x[:pad], x[TR - pad:]
        one_ref[at:at + pad] = jnp.where(even, last, first)
        two_ref[at:at + pad] = jnp.where(even, first, last)
        at += pad


def _weights(w1_ref, w2_ref, bias_ref, m1_ref, m2_ref, b_ref, w1, w2, flat, sems):
    _fetch([(w1_ref, w1), (w2_ref, w2)], sems)
    lane = lax.broadcasted_iota(jnp.int32, (CH, 128), 1)
    sub = lax.broadcasted_iota(jnp.int32, (CH, 128), 0)
    flat[0] = jnp.zeros((CH, 128), jnp.float32)
    flat[1] = jnp.zeros((CH, 128), jnp.float32)
    flat[0, :, 0:9] = w1[...]
    for c2 in range(CH):
        flat[1, :, 9 * c2:9 * c2 + 9] = w2[:, c2, :]
    b = jnp.zeros((CH, 128), jnp.float32)
    for c in range(CH):
        b = jnp.where(sub == c, bias_ref[c], b)
    b_ref[...] = b
    hi_rows, lo_rows = [], []
    for y in range(8):
        ky = lane % 16 - y - (HALO_PAD - HALO_M)
        v = _pick(flat[0], jnp.clip(3 * ky + lane // 16, 0, 127))
        v = jnp.where((ky >= 0) & (ky <= 2), v, 0.0)
        hi = v.astype(jnp.bfloat16).astype(jnp.float32)
        hi_rows.append(hi)
        lo_rows.append(v - hi)
    m1_ref[...] = jnp.concatenate(hi_rows + lo_rows, axis=0)[:, :48].astype(jnp.bfloat16)
    hi_rows, lo_rows = [], []
    for kx in range(3):
        for y in range(8):
            halves = []
            for half in range(2):
                at = lane + 128 * half
                at = jnp.where(at >= 80, at - 80, at)
                ky = at // 8 - y
                v = _pick(flat[1], jnp.clip(9 * (at % 8) + 3 * ky + kx, 0, 127))
                halves.append(jnp.where((ky >= 0) & (ky <= 2), v, 0.0))
            v = jnp.concatenate(halves, axis=1)
            hi = v.astype(jnp.bfloat16).astype(jnp.float32)
            wide = lax.broadcasted_iota(jnp.int32, (CH, 256), 1)
            hi_rows.append(hi)
            lo_rows.append(jnp.where(wide < 80, v - hi, 0.0))
    m2_ref[...] = jnp.concatenate(hi_rows + lo_rows, axis=0)[:, :160].astype(jnp.bfloat16)


def _pack_cols(own_ref, up_ref, down_ref, one_ref, two_ref):
    even = lax.rem(lax.axis_index("col"), 2) == 0
    tall = _tall(_own(own_ref), up_ref[...], down_ref[...])
    lane = lax.broadcasted_iota(jnp.int32, (8, 128), 1)
    for i in range(TALL // 8):
        first = last = None
        for k in (3, 2, 1, 0):
            if 8 * i < tall[k].shape[0]:
                v = tall[k][8 * i:8 * i + 8]
                a, b = _roll(v, 32 * k, 1), _roll(v, 32 * k + HALO_M, 1)
                first = a if first is None else jnp.where(lane < 32 * k + 32, a, first)
                last = b if last is None else jnp.where(lane < 32 * k + 32, b, last)
        one_ref[8 * i:8 * i + 8] = jnp.where(even, last, first)
        two_ref[8 * i:8 * i + 8] = jnp.where(even, first, last)


def _windows(own, up, down, one, two):
    c, n = lax.axis_index("col"), lax.axis_size("col")
    even = lax.rem(c, 2) == 0
    left = jnp.where(c > 0, jnp.where(even, two, one), 0.0)
    right = jnp.where(c < n - 1, jnp.where(even, one, two), 0.0)
    out = []
    end = HALO_M - HALF + TC
    for k, x in enumerate(_tall(own, up, down)):
        lane = lax.broadcasted_iota(jnp.int32, x.shape, 1)
        r = x.shape[0]
        lw = jnp.where(lane < HALO_M, _roll(left[:r], -32 * k, 1), _roll(x, HALO_M, 1))
        rw = jnp.where(lane < end, _roll(x, HALO_M - HALF, 1), _roll(right[:r], end - 32 * k, 1))
        out.append((lw, rw))
    return out


def _kernel(own_ref, up_ref, down_ref, one_ref, two_ref, w1_ref, bias_ref, w2_ref, out_ref,
            hs, e3, ef, raw, m1, m2, sq, disp, frac, idx, dat):
    row0, col0 = TR * lax.axis_index("row"), TC * lax.axis_index("col")
    rows, cols = TR * lax.axis_size("row"), TC * lax.axis_size("col")
    lane = lax.broadcasted_iota(jnp.int32, (CH, 128), 1)
    col_ok = []
    for h in range(2):
        c = col0 + HALF * h - LANE0 + lane
        col_ok.append((c >= 0) & (c < cols))
    bias = bias_ref[...]
    moving, fixed, *field = _windows(
        _own(own_ref), up_ref[...], down_ref[...], one_ref[...], two_ref[...])
    def keep(y, h):
        r = row0 + y
        ok = jnp.where((r >= 0) & (r < rows), 1, 0)
        return jnp.where(col_ok[h], ok.astype(jnp.float32), 0.0)

    def embed(image, top, blocks, sink):
        shifted = [jnp.concatenate([_roll(image[h], 1 - kx, 1) for h in range(2)], axis=1) for kx in range(3)]
        known = image[0].shape[0]
        for b in range(blocks + 1):
            if 8 * b + 16 > known:
                for k in range(8 * b, 8 * blocks + 2, 2):
                    hs[0, CH * k:CH * k + 16] = jnp.zeros((16, 256), jnp.bfloat16)
                    hs[1, CH * k:CH * k + 16] = jnp.zeros((16, 256), jnp.bfloat16)
                break
            t = _dot(w1_ref[...], jnp.concatenate([x[8 * b:8 * b + 16] for x in shifted], axis=0).astype(jnp.bfloat16))
            pre = t[:64] + t[64:]
            for h in range(2):
                v = jnp.concatenate([
                    jnp.maximum(pre[CH * k:CH * k + CH, 128 * h:128 * h + 128] + bias, 0.0) * keep(top - 1 + 8 * b + k, h)
                    for k in range(8)], axis=0)
                hi, lo = _split(v)
                hs[0, 64 * b:64 * b + 64, 128 * h:128 * h + 128] = hi
                hs[1, 64 * b:64 * b + 64, 128 * h:128 * h + 128] = lo
        for b in range(blocks):
            t = _dot(w2_ref[...], jnp.concatenate([hs[0, 64 * b:64 * b + 80], hs[1, 64 * b:64 * b + 80]], axis=0))
            v = t[:192] + t[192:]
            for h in range(2):
                o = [v[64 * kx:64 * kx + 64, 128 * h:128 * h + 128] for kx in range(3)]
                e = o[1] + _roll(o[0], 1, 1) + _roll(o[2], -1, 1)
                sink(b, h, [e[CH * k:CH * k + CH] * keep(top + 8 * b + k, h) for k in range(8)])

    fixed_rows = [[], []]

    def fixed_sink(b, h, got):
        fixed_rows[h].extend(got)

    embed(fixed, -3, FE_BLOCKS, fixed_sink)
    for s in range(SEGS):
        h, first = _segment(s)
        for q in range(NQ):
            cur = None
            for i in range(4):
                row = min(max(4 * q - 1 + i, 0), 8 * FE_BLOCKS - 1)
                v = _roll(fixed_rows[h][row], 32 * i - (WIDE * s - SIDE - first), 1)
                cur = v if i == 0 else jnp.where(lane < 32 * i, cur, v)
            ef[s, q] = cur

    moving_rows = [[], []]

    def moving_sink(b, h, got):
        moving_rows[h].extend(got)

    embed(moving, -(REACH + 3), ME_BLOCKS, moving_sink)
    for r in range(0, PROWS, 2):
        for s in range(SEGS):
            h, first = _segment(s)
            at = WIDE * s - 3 - REACH - first
            out = []
            for k in (r, r + 1):
                e0 = jnp.where(lane < 64, _roll(moving_rows[h][k], -at, 1), _roll(moving_rows[h][k + CUT], 64 - at, 1))
                left, right = _roll(e0, 1, 1), _roll(e0, -1, 1)
                p1 = 0.5 * (right - left)
                p2 = 0.5 * (right + left) - e0
                out += [e0 + 0.25 * p2, p1, p2]
            hi, lo = _split(jnp.concatenate(out, axis=0))
            e3[s, 24 * r:24 * r + 48, 0:128] = hi
            e3[s, 24 * r:24 * r + 48, 128:256] = lo

    sub = lax.broadcasted_iota(jnp.int32, (8, 128), 0)
    mine = lane // 32 == sub % 4
    raw[...] = jnp.zeros_like(raw)
    for comp in range(2):
        for b in range(NQ // 2):
            for s in range(SEGS):
                h, first = _segment(s)
                v = field[comp][h][8 * b + 4:8 * b + 12]
                v = _pick(v, (lane - 32 * (sub % 4) + (WIDE * s - SIDE - first)) & 127)
                for k in range(2):
                    raw[comp, 2 * b + k, s:s + 1, :] = jnp.sum(
                        jnp.where(mine & (sub // 4 == k), v, 0.0), axis=0, keepdims=True)
    m1[...] = jnp.zeros_like(m1)
    m2[...] = jnp.zeros_like(m2)
    dat[...] = jnp.zeros_like(dat)

    j = lane % 32
    x = col0 + WIDE * sub - SIDE + j
    col_in = (x >= 0) & (x < cols)
    iota_k = lax.broadcasted_iota(jnp.int32, (128, 256), 0).astype(jnp.float32).astype(jnp.bfloat16)

    def group(q0, s):
        start = max(4 * q0 - 4, -2) + 2

        def pair(ref, comp, count):
            return jnp.concatenate(
                [jnp.broadcast_to(ref[comp, q0 + k, s:s + 1, :], (count, 128)) for k in range(2)], axis=1)

        col = pair(idx, 1, 1) + jnp.where(pair(idx, 0, 1) >= start + CUT, 64.0, 0.0)
        pick = jnp.where(iota_k == jnp.broadcast_to(col.astype(jnp.bfloat16), (128, 256)),
                         jnp.bfloat16(1.0), jnp.bfloat16(0.0))
        count = CUT + 2
        t = _dot(e3[s, 24 * start:24 * (start + count), :], jnp.concatenate([pick, pick], axis=0))
        base = pair(idx, 0, 8) - (start * 1.0)
        base = jnp.where(base >= CUT, base - CUT, base)
        conds = []
        for cut in _levels(CUT):
            c = base >= cut
            conds.append((cut, c))
            base = jnp.where(c, base - cut, base)
        taps = []
        for b in range(3):
            T = [t[24 * k + 8 * b:24 * k + 8 * b + 8] for k in range(count)]
            for cut, c in conds:
                T = [jnp.where(c, T[k + cut], T[k]) if k + cut < len(T) else T[k] for k in range(cut + 2)]
            taps.append(T)
        fr, fc = pair(frac, 0, 8), pair(frac, 1, 8)
        A, B = [], []
        for a in range(3):
            w = fc * taps[2][a]
            v = taps[1][a] + w
            A.append(taps[0][a] + fc * v)
            B.append(v + w)
        da, qa = 0.5 * (A[2] - A[0]), 0.5 * (A[2] + A[0]) - A[1]
        db, qb = 0.5 * (B[2] - B[0]), 0.5 * (B[2] + B[0]) - B[1]
        wa = fr * qa
        va = da + wa
        warped = A[1] + 0.25 * qa + fr * va
        slope_row = va + wa
        slope_col = B[1] + 0.25 * qb + fr * (db + fr * qb)
        target = jnp.concatenate([ef[s, q0], ef[s, q0 + 1]], axis=1)
        miss = (warped - target) * (2.0 / CH)
        for comp, slope in ((0, slope_row), (1, slope_col)):
            total = jnp.sum(miss * slope, axis=0, keepdims=True)
            for k in range(2):
                dat[comp, q0 + k, s:s + 1, :] = total[:, 128 * k:128 * k + 128]

    def step(t):
        for q in range(NQ):
            y = 4 * q - 4 + lane // 32
            ok = col_in & (row0 + y >= 0) & (row0 + y < rows)
            for comp, origin in ((0, y + REACH + 2), (1, j + REACH)):
                v = jnp.tanh(raw[comp, q] * (1.0 / REACH))
                d = REACH * v
                n = jnp.floor(d + 0.5)
                sq[comp, q] = v
                disp[comp, q] = jnp.where(ok, d, 0.0)
                frac[comp, q] = d - n
                idx[comp, q] = n + origin.astype(jnp.float32)
        for q0 in range(0, NQ, 2) if t < 2 else range(1, NQ - 1, 2):
            for s in range(SEGS):
                group(q0, s)
        one, two = 1.0 / (1.0 - 0.9 ** (t + 1)), 1.0 / (1.0 - 0.999 ** (t + 1))
        for comp in range(2):
            for q in range(NQ) if t < 2 else range(1, NQ - 1):
                d = disp[comp, q]
                up = jnp.where(lane < 96, _roll(d, -32, 1), _roll(disp[comp, min(q + 1, NQ - 1)], -32, 1))
                down = jnp.where(lane >= 32, _roll(d, 32, 1), _roll(disp[comp, max(q - 1, 0)], 32, 1))
                around = up + down + _roll(d, 1, 1) + _roll(d, -1, 1)
                v = sq[comp, q]
                grad = (dat[comp, q] + 2.0 * STIFFNESS * (4.0 * REACH * v - around)) * (1.0 - v * v)
                a = 0.9 * m1[comp, q] + 0.1 * grad
                b = 0.999 * m2[comp, q] + 0.001 * grad * grad
                m1[comp, q] = a
                m2[comp, q] = b
                raw[comp, q] = raw[comp, q] - STEP * (a * one) / (jnp.sqrt(b * two) + EPS)

    for t in range(ITERS):
        step(t)

    own = _own(own_ref)
    for comp in range(2):
        for b in range(TR // 8):
            out = None
            for s in range(SEGS):
                v = jnp.where(sub < 4, jnp.broadcast_to(raw[comp, 2 * b + 1, s:s + 1, :], (8, 128)),
                              jnp.broadcast_to(raw[comp, 2 * b + 2, s:s + 1, :], (8, 128)))
                v = _pick(v, (lane + 32 * (sub % 4) + (128 + SIDE - WIDE * s)) & 127)
                out = v if s == 0 else jnp.where(lane < WIDE * s, out, v)
            out_ref[comp, 8 * b:8 * b + 8] = out - own[2 + comp][8 * b:8 * b + 8]


def _swaps(n, first):
    return [p for a in range(first, n, 2) for p in ((a, (a + 1) % n), ((a + 1) % n, a))]


def _exchange(pair, axis):
    n = lax.axis_size(axis)
    return [lax.ppermute(x, axis, _swaps(n, k)) for k, x in enumerate(pair)]


def _local(fixed_section, moving_section, field_init, first_weight, first_bias, second_weight):
    vmem = pl.BlockSpec(memory_space=pltpu.VMEM)
    smem = pl.BlockSpec(memory_space=pltpu.SMEM)
    anywhere = pl.BlockSpec(memory_space=pltpu.HBM)
    f32, bf16 = jnp.float32, jnp.bfloat16

    def call(body, name, out, specs, scratch):
        return pl.pallas_call(
            body,
            out_shape=[jax.ShapeDtypeStruct(*x) for x in out],
            in_specs=specs,
            out_specs=[vmem] * len(out),
            scratch_shapes=scratch,
            compiler_params=pltpu.CompilerParams(vmem_limit_bytes=48 * 2 ** 20),
            name=name,
        )

    strip = ((sum(PADS), 128), f32)
    one, two, own = call(_pack_rows, "pack_rows", [strip, strip, ((4 * TR, TC), f32)], [anywhere] * 3, [
        pltpu.VMEM((TR, TC), bf16), pltpu.VMEM((TR, TC), bf16), pltpu.VMEM((2, TR, TC), f32),
        pltpu.SemaphoreType.DMA((3,))])(*[pltpu.with_memory_space_constraint(x, pltpu.HBM) for x in (moving_section, fixed_section, field_init)])
    up, down = _exchange((one, two), "row")
    w1, w2, bias = call(_weights, "weights", [((128, 48), bf16), ((384, 160), bf16), ((CH, 128), f32)],
                        [anywhere, anywhere, smem], [
        pltpu.VMEM((CH, 9), f32), pltpu.VMEM((CH, CH, 9), f32), pltpu.VMEM((2, CH, 128), f32),
        pltpu.SemaphoreType.DMA((2,))])(first_weight, second_weight, first_bias)
    strip = ((TALL, 128), f32)
    one, two = _exchange(call(_pack_cols, "pack_cols", [strip, strip], [vmem] * 3, [])(own, up, down), "col")
    return call(_kernel, "refine", [((2, TR, TC), f32)], [vmem] * 8, [
        pltpu.VMEM((2, HROWS * CH, 256), bf16),
        pltpu.VMEM((SEGS, PROWS * 24, 256), bf16),
        pltpu.VMEM((SEGS, NQ, CH, 128), f32),
        *[pltpu.VMEM((2, NQ, 8, 128), f32) for _ in range(8)],
    ])(own, up, down, one, two, w1, bias, w2)[0]


def solution(mesh):
    return jax.shard_map(
        _local,
        mesh=mesh,
        in_specs=(P("row", "col"), P("row", "col"), P(None, "row", "col"), P(), P(), P()),
        out_specs=P(None, "row", "col"),
        check_vma=False,
    )
```

```python
import jax
import jax.numpy as jnp
from jax import lax
from jax.experimental import pallas as pl
from jax.experimental.pallas import tpu as pltpu
from jax.sharding import PartitionSpec as P

CH = 8
REACH = 16
ITERS = 3
STIFFNESS = 0.01
STEP = 0.5
EPS = 0.01

TR, TC = 32, 128
SIDE = 3
HALO_M = REACH + 1 + 2 + 2
HALO_PAD = 24
PADS = (HALO_PAD, 8, 8, 8)
TALL = TR + 2 * HALO_PAD
EROWS = 72
HROWS = 80
TOP = -(REACH + 3)
BLOCKS = EROWS // 8
FIXED_BLOCKS = range(2, 7)

SEGS = 5
WIDE = 26
NQ = 10
CUT = 20
PROWS = EROWS - CUT


FROM0 = REACH + 3
AT4 = 62
FROM4 = WIDE * (SEGS - 1) - FROM0 - AT4


def _levels(span):
    out = []
    while span > 1:
        cut = (span + 1) // 2
        out.append(cut)
        span = cut
    return out


def _split(x):
    hi = x.astype(jnp.bfloat16)
    lo = (x - hi.astype(jnp.float32)).astype(jnp.bfloat16)
    return hi, lo


def _roll(x, shift, axis):
    size = x.shape[axis]
    shift = shift % size
    return x if shift == 0 else pltpu.roll(x, shift, axis)


def _pick(x, index):
    dims = lax.GatherDimensionNumbers(
        offset_dims=(), collapsed_slice_dims=(1,), start_index_map=(1,),
        operand_batching_dims=(0,), start_indices_batching_dims=(0,))
    return lax.gather(x, index[..., None], dims, (1, 1), mode=lax.GatherScatterMode.PROMISE_IN_BOUNDS)


def _dot(a, b):
    return jnp.dot(a, b, preferred_element_type=jnp.float32)


def _tall(own, one, two):
    r, n = lax.axis_index("row"), lax.axis_size("row")
    even = lax.rem(r, 2) == 0
    above = jnp.where(r > 0, jnp.where(even, two, one), 0.0)
    below = jnp.where(r < n - 1, jnp.where(even, one, two), 0.0)
    out, at = [], 0
    for x, pad in zip(own, PADS):
        out.append(jnp.concatenate([above[at:at + pad], x, below[at:at + pad]], axis=0))
        at += pad
    return out


def _fetch(pairs, sems):
    copies = [pltpu.make_async_copy(src, dst, sems.at[k]) for k, (src, dst) in enumerate(pairs)]
    for copy in copies:
        copy.start()
    for copy in copies:
        copy.wait()


def _own(own_ref):
    return [own_ref[TR * k:TR * k + TR] for k in range(4)]


def _pack_rows(mv_ref, fx_ref, fd_ref, one_ref, two_ref, own_ref, mv, fx, fd, sems):
    _fetch([(mv_ref, mv), (fx_ref, fx), (fd_ref, fd)], sems)
    even = lax.rem(lax.axis_index("row"), 2) == 0
    at = 0
    for k, x in enumerate([mv[...].astype(jnp.float32), fx[...].astype(jnp.float32), fd[0], fd[1]]):
        pad = PADS[k]
        own_ref[TR * k:TR * k + TR] = x
        first, last = x[:pad], x[TR - pad:]
        one_ref[at:at + pad] = jnp.where(even, last, first)
        two_ref[at:at + pad] = jnp.where(even, first, last)
        at += pad


def _weights(w1_ref, w2_ref, bias_ref, m1_ref, m2_ref, b_ref, w1, w2, flat, sems):
    _fetch([(w1_ref, w1), (w2_ref, w2)], sems)
    lane = lax.broadcasted_iota(jnp.int32, (CH, 128), 1)
    sub = lax.broadcasted_iota(jnp.int32, (CH, 128), 0)
    flat[0] = jnp.zeros((CH, 128), jnp.float32)
    flat[1] = jnp.zeros((CH, 128), jnp.float32)
    flat[0, :, 0:9] = w1[...]
    for c2 in range(CH):
        flat[1, :, 9 * c2:9 * c2 + 9] = w2[:, c2, :]
    b = jnp.zeros((CH, 128), jnp.float32)
    for c in range(CH):
        b = jnp.where(sub == c, bias_ref[c], b)
    b_ref[...] = b
    hi_rows, lo_rows = [], []
    for y in range(8):
        ky = lane % 16 - y - (HALO_PAD - HALO_M)
        v = _pick(flat[0], jnp.clip(3 * ky + lane // 16, 0, 127))
        v = jnp.where((ky >= 0) & (ky <= 2), v, 0.0)
        hi = v.astype(jnp.bfloat16).astype(jnp.float32)
        hi_rows.append(hi)
        lo_rows.append(v - hi)
    m1_ref[...] = jnp.concatenate(hi_rows + lo_rows, axis=0)[:, :48].astype(jnp.bfloat16)
    hi_rows, lo_rows = [], []
    for kx in range(3):
        for y in range(8):
            halves = []
            for half in range(2):
                at = lane + 128 * half
                at = jnp.where(at >= 80, at - 80, at)
                ky = at // 8 - y
                v = _pick(flat[1], jnp.clip(9 * (at % 8) + 3 * ky + kx, 0, 127))
                halves.append(jnp.where((ky >= 0) & (ky <= 2), v, 0.0))
            v = jnp.concatenate(halves, axis=1)
            hi = v.astype(jnp.bfloat16).astype(jnp.float32)
            wide = lax.broadcasted_iota(jnp.int32, (CH, 256), 1)
            hi_rows.append(hi)
            lo_rows.append(jnp.where(wide < 80, v - hi, 0.0))
    m2_ref[...] = jnp.concatenate(hi_rows + lo_rows, axis=0)[:, :160].astype(jnp.bfloat16)


def _pack_cols(own_ref, up_ref, down_ref, _, one_ref, two_ref):
    even = lax.rem(lax.axis_index("col"), 2) == 0
    tall = _tall(_own(own_ref), up_ref[...], down_ref[...])
    lane = lax.broadcasted_iota(jnp.int32, (8, 128), 1)
    for i in range(TALL // 8):
        first = last = None
        for k in (3, 2, 1, 0):
            if 8 * i < tall[k].shape[0]:
                v = tall[k][8 * i:8 * i + 8]
                a, b = _roll(v, 32 * k, 1), _roll(v, 32 * k + HALO_M, 1)
                first = a if first is None else jnp.where(lane < 32 * k + 32, a, first)
                last = b if last is None else jnp.where(lane < 32 * k + 32, b, last)
        one_ref[8 * i:8 * i + 8] = jnp.where(even, last, first)
        two_ref[8 * i:8 * i + 8] = jnp.where(even, first, last)


def _strips(own, up, down, one, two):
    c, n = lax.axis_index("col"), lax.axis_size("col")
    even = lax.rem(c, 2) == 0
    left = jnp.where(c > 0, jnp.where(even, two, one), 0.0)
    right = jnp.where(c < n - 1, jnp.where(even, one, two), 0.0)
    out = []
    for k, x in enumerate(_tall(own, up, down)):
        lane = lax.broadcasted_iota(jnp.int32, x.shape, 1)
        r = x.shape[0]
        v = jnp.where(lane < TC - FROM4, _roll(x, -FROM4, 1), _roll(right[:r], TC - FROM4 - 32 * k, 1))
        v = jnp.where(lane < AT4, _roll(x, FROM0, 1), v)
        out.append(jnp.where((lane < FROM0) | (lane >= 126), _roll(left[:r], FROM0 - HALO_M - 32 * k, 1), v))
    return out


class _Place:
    def __init__(self):
        self.row, self.col = TR * lax.axis_index("row"), TC * lax.axis_index("col")
        self.rows, self.cols = TR * lax.axis_size("row"), TC * lax.axis_size("col")

    def keep(self, y, col_ok):
        r = self.row + y
        ok = jnp.where((r >= 0) & (r < self.rows), 1, 0)
        return jnp.where(col_ok, ok.astype(jnp.float32), 0.0)


def _embed(place, moving, fixed, column, w1_ref, bias_ref, w2_ref, hs, sink):
    bias = bias_ref[...]
    x = place.col + column
    col_ok = (x >= 0) & (x < place.cols)
    blank = jnp.zeros((16, 128), jnp.float32)
    image = [moving, jnp.concatenate([blank, fixed, blank], axis=0)]
    shifted = [jnp.concatenate([_roll(v, 1 - kx, 1) for v in image], axis=1) for kx in range(3)]
    hs[:, 8 * 72:, :] = jnp.zeros((2, 64, 256), jnp.bfloat16)
    for b in range(BLOCKS):
        t = _dot(w1_ref[...], jnp.concatenate([v[8 * b:8 * b + 16] for v in shifted], axis=0).astype(jnp.bfloat16))
        pre = t[:64] + t[64:]
        for h in range(2):
            at = slice(128 * h, 128 * h + 128)
            if h == 1 and b not in FIXED_BLOCKS:
                hs[:, 64 * b:64 * b + 64, at] = jnp.zeros((2, 64, 128), jnp.bfloat16)
                continue
            v = jnp.concatenate([
                jnp.maximum(pre[CH * k:CH * k + CH, at] + bias, 0.0) * place.keep(TOP - 1 + 8 * b + k, col_ok)
                for k in range(8)], axis=0)
            hs[0, 64 * b:64 * b + 64, at], hs[1, 64 * b:64 * b + 64, at] = _split(v)
    for b in range(BLOCKS):
        t = _dot(w2_ref[...], jnp.concatenate([hs[0, 64 * b:64 * b + 80], hs[1, 64 * b:64 * b + 80]], axis=0))
        v = t[:192] + t[192:]
        for h in range(2):
            if h == 1 and b not in FIXED_BLOCKS:
                continue
            o = [v[64 * kx:64 * kx + 64, 128 * h:128 * h + 128] for kx in range(3)]
            e = o[1] + _roll(o[0], 1, 1) + _roll(o[2], -1, 1)
            sink(b, h, [e[CH * k:CH * k + CH] * place.keep(TOP + 8 * b + k, col_ok) for k in range(8)])


def _build(moving, fixed, field, window, pixel, s, e3, ef, raw):
    lane = lax.broadcasted_iota(jnp.int32, (8, 128), 1)
    sub = lax.broadcasted_iota(jnp.int32, (8, 128), 0)
    mine = lane // 32 == sub % 4
    for r in range(0, PROWS, 2):
        out = []
        for k in (r, r + 1):
            e0 = jnp.where(lane < 64, _roll(moving[k], -window, 1), _roll(moving[k + CUT], 64 - window, 1))
            left, right = _roll(e0, 1, 1), _roll(e0, -1, 1)
            p1 = 0.5 * (right - left)
            p2 = 0.5 * (right + left) - e0
            out += [e0 + 0.25 * p2, p1, p2]
        hi, lo = _split(jnp.concatenate(out, axis=0))
        e3[24 * r:24 * r + 48, 0:128] = hi
        e3[24 * r:24 * r + 48, 128:256] = lo
    for q in range(NQ):
        cur = None
        for i in range(4):
            row = min(max(4 * q - 4 + i, -2), TR + 1) - TOP
            v = _roll(fixed[row], 32 * i - pixel, 1)
            cur = v if i == 0 else jnp.where(lane < 32 * i, cur, v)
        ef[q] = cur
    for comp in range(2):
        for b in range(NQ // 2):
            v = field[comp][8 * b + 4:8 * b + 12]
            v = _pick(v, (lane - 32 * (sub % 4) + pixel) & 127)
            for k in range(2):
                raw[comp, 2 * b + k, s:s + 1, :] = jnp.sum(
                    jnp.where(mine & (sub // 4 == k), v, 0.0), axis=0, keepdims=True)


def _middle(own_ref, up_ref, down_ref, w1_ref, bias_ref, w2_ref, e3_ref, ef_ref, raw_ref, rows_ref, hs):
    moving, fixed, *field = _tall(_own(own_ref), up_ref[...], down_ref[...])
    lane = lax.broadcasted_iota(jnp.int32, (CH, 128), 1)
    rows = [{}, {}]

    def sink(b, h, got):
        for k, v in enumerate(got):
            rows[h][8 * b + k] = v
            rows_ref[h, 8 * b + k] = v

    _embed(_Place(), moving, fixed, lane, w1_ref, bias_ref, w2_ref, hs, sink)
    raw_ref[...] = jnp.zeros_like(raw_ref)
    for s in range(1, SEGS - 1):
        _build(rows[0], rows[1], field, WIDE * s - 3 - REACH, WIDE * s - SIDE, s,
               e3_ref.at[s - 1], ef_ref.at[s - 1], raw_ref)


def _refine(own_ref, up_ref, down_ref, one_ref, two_ref, w1_ref, bias_ref, w2_ref, mid3_ref, midf_ref, midr_ref, rows_ref,
            out_ref, hs, e3, ef, raw, m1, m2, sq, disp, frac, idx, dat):
    place = _Place()
    row0, col0, rows, cols = place.row, place.col, place.rows, place.cols
    lane = lax.broadcasted_iota(jnp.int32, (8, 128), 1)
    sub = lax.broadcasted_iota(jnp.int32, (8, 128), 0)
    moving, fixed, *field = _strips(_own(own_ref), up_ref[...], down_ref[...], one_ref[...], two_ref[...])
    column = jnp.where(lane < AT4, lane - FROM0, jnp.where(lane < 126, lane + FROM4, lane - 126 - HALO_M))
    edge = [[{}, {}], [{}, {}]]

    def sink(b, h, got):
        for k, v in enumerate(got):
            mine = rows_ref[h, 8 * b + k]
            edge[0][h][8 * b + k] = jnp.where(lane < 30, v, _roll(mine, FROM0, 1))
            edge[1][h][8 * b + k] = jnp.where(lane < 90, _roll(mine, -FROM4, 1), v)

    _embed(place, moving, fixed, column, w1_ref, bias_ref, w2_ref, hs, sink)
    raw[...] = midr_ref[...]
    _build(edge[0][0], edge[0][1], field, 0, REACH, 0, e3.at[0], ef.at[0], raw)
    _build(edge[1][0], edge[1][1], field, AT4, AT4 + REACH, SEGS - 1, e3.at[1], ef.at[1], raw)
    tables = [e3.at[0]] + [mid3_ref.at[k] for k in range(SEGS - 2)] + [e3.at[1]]
    targets = [ef.at[0]] + [midf_ref.at[k] for k in range(SEGS - 2)] + [ef.at[1]]
    m1[...] = jnp.zeros_like(m1)
    m2[...] = jnp.zeros_like(m2)
    dat[...] = jnp.zeros_like(dat)

    j = lane % 32
    x = col0 + WIDE * sub - SIDE + j
    col_in = (x >= 0) & (x < cols)
    iota_k = lax.broadcasted_iota(jnp.int32, (128, 256), 0).astype(jnp.float32).astype(jnp.bfloat16)

    def group(q0, s):
        start = max(4 * q0 - 4, -2) + 2

        def pair(ref, comp, count):
            return jnp.concatenate(
                [jnp.broadcast_to(ref[comp, q0 + k, s:s + 1, :], (count, 128)) for k in range(2)], axis=1)

        col = pair(idx, 1, 1) + jnp.where(pair(idx, 0, 1) >= start + CUT, 64.0, 0.0)
        pick = jnp.where(iota_k == jnp.broadcast_to(col.astype(jnp.bfloat16), (128, 256)),
                         jnp.bfloat16(1.0), jnp.bfloat16(0.0))
        count = CUT + 2
        t = _dot(tables[s][24 * start:24 * (start + count), :], jnp.concatenate([pick, pick], axis=0))
        base = pair(idx, 0, 8) - (start * 1.0)
        base = jnp.where(base >= CUT, base - CUT, base)
        conds = []
        for cut in _levels(CUT):
            c = base >= cut
            conds.append((cut, c))
            base = jnp.where(c, base - cut, base)
        taps = []
        for b in range(3):
            T = [t[24 * k + 8 * b:24 * k + 8 * b + 8] for k in range(count)]
            for cut, c in conds:
                T = [jnp.where(c, T[k + cut], T[k]) if k + cut < len(T) else T[k] for k in range(cut + 2)]
            taps.append(T)
        fr, fc = pair(frac, 0, 8), pair(frac, 1, 8)
        A, B = [], []
        for a in range(3):
            w = fc * taps[2][a]
            v = taps[1][a] + w
            A.append(taps[0][a] + fc * v)
            B.append(v + w)
        da, qa = 0.5 * (A[2] - A[0]), 0.5 * (A[2] + A[0]) - A[1]
        db, qb = 0.5 * (B[2] - B[0]), 0.5 * (B[2] + B[0]) - B[1]
        wa = fr * qa
        va = da + wa
        warped = A[1] + 0.25 * qa + fr * va
        slope_row = va + wa
        slope_col = B[1] + 0.25 * qb + fr * (db + fr * qb)
        target = jnp.concatenate([targets[s][q0], targets[s][q0 + 1]], axis=1)
        miss = (warped - target) * (2.0 / CH)
        for comp, slope in ((0, slope_row), (1, slope_col)):
            total = jnp.sum(miss * slope, axis=0, keepdims=True)
            for k in range(2):
                dat[comp, q0 + k, s:s + 1, :] = total[:, 128 * k:128 * k + 128]

    def step(t):
        for q in range(NQ):
            y = 4 * q - 4 + lane // 32
            ok = col_in & (row0 + y >= 0) & (row0 + y < rows)
            for comp, origin in ((0, y + REACH + 2), (1, j + REACH)):
                v = jnp.tanh(raw[comp, q] * (1.0 / REACH))
                d = REACH * v
                n = jnp.floor(d + 0.5)
                sq[comp, q] = v
                disp[comp, q] = jnp.where(ok, d, 0.0)
                frac[comp, q] = d - n
                idx[comp, q] = n + origin.astype(jnp.float32)
        for q0 in range(0, NQ, 2) if t < 2 else range(1, NQ - 1, 2):
            for s in range(SEGS):
                group(q0, s)
        one, two = 1.0 / (1.0 - 0.9 ** (t + 1)), 1.0 / (1.0 - 0.999 ** (t + 1))
        for comp in range(2):
            for q in range(NQ) if t < 2 else range(1, NQ - 1):
                d = disp[comp, q]
                up = jnp.where(lane < 96, _roll(d, -32, 1), _roll(disp[comp, min(q + 1, NQ - 1)], -32, 1))
                down = jnp.where(lane >= 32, _roll(d, 32, 1), _roll(disp[comp, max(q - 1, 0)], 32, 1))
                around = up + down + _roll(d, 1, 1) + _roll(d, -1, 1)
                v = sq[comp, q]
                grad = (dat[comp, q] + 2.0 * STIFFNESS * (4.0 * REACH * v - around)) * (1.0 - v * v)
                a = 0.9 * m1[comp, q] + 0.1 * grad
                b = 0.999 * m2[comp, q] + 0.001 * grad * grad
                m1[comp, q] = a
                m2[comp, q] = b
                raw[comp, q] = raw[comp, q] - STEP * (a * one) / (jnp.sqrt(b * two) + EPS)

    for t in range(ITERS):
        step(t)

    own = _own(own_ref)
    for comp in range(2):
        for b in range(TR // 8):
            out = None
            for s in range(SEGS):
                v = jnp.where(sub < 4, jnp.broadcast_to(raw[comp, 2 * b + 1, s:s + 1, :], (8, 128)),
                              jnp.broadcast_to(raw[comp, 2 * b + 2, s:s + 1, :], (8, 128)))
                v = _pick(v, (lane + 32 * (sub % 4) + (128 + SIDE - WIDE * s)) & 127)
                out = v if s == 0 else jnp.where(lane < WIDE * s, out, v)
            out_ref[comp, 8 * b:8 * b + 8] = out - own[2 + comp][8 * b:8 * b + 8]


def _swaps(n, first):
    return [p for a in range(first, n, 2) for p in ((a, (a + 1) % n), ((a + 1) % n, a))]


def _exchange(pair, axis):
    n = lax.axis_size(axis)
    return [lax.ppermute(x, axis, _swaps(n, k)) for k, x in enumerate(pair)]


def _local(fixed_section, moving_section, field_init, first_weight, first_bias, second_weight):
    vmem = pl.BlockSpec(memory_space=pltpu.VMEM)
    smem = pl.BlockSpec(memory_space=pltpu.SMEM)
    anywhere = pl.BlockSpec(memory_space=pltpu.HBM)
    f32, bf16 = jnp.float32, jnp.bfloat16

    def call(body, name, out, specs, scratch):
        return pl.pallas_call(
            body,
            out_shape=[jax.ShapeDtypeStruct(*x) for x in out],
            in_specs=specs,
            out_specs=[vmem] * len(out),
            scratch_shapes=scratch,
            compiler_params=pltpu.CompilerParams(vmem_limit_bytes=48 * 2 ** 20),
            name=name,
        )

    strip = ((sum(PADS), 128), f32)
    one, two, own = call(_pack_rows, "pack_rows", [strip, strip, ((4 * TR, TC), f32)], [anywhere] * 3, [
        pltpu.VMEM((TR, TC), bf16), pltpu.VMEM((TR, TC), bf16), pltpu.VMEM((2, TR, TC), f32),
        pltpu.SemaphoreType.DMA((3,))])(*[pltpu.with_memory_space_constraint(x, pltpu.HBM) for x in (moving_section, fixed_section, field_init)])
    up, down = _exchange((one, two), "row")
    w1, w2, bias = call(_weights, "weights", [((128, 48), bf16), ((384, 160), bf16), ((CH, 128), f32)],
                        [anywhere, anywhere, smem], [
        pltpu.VMEM((CH, 9), f32), pltpu.VMEM((CH, CH, 9), f32), pltpu.VMEM((2, CH, 128), f32),
        pltpu.SemaphoreType.DMA((2,))])(first_weight, second_weight, first_bias)
    strip = ((TALL, 128), f32)
    one, two = _exchange(call(_pack_cols, "pack_cols", [strip, strip], [vmem] * 4, [])(own, up, down, bias), "col")
    hidden = pltpu.VMEM((2, HROWS * CH, 256), bf16)
    table, target = (PROWS * 24, 256), (NQ, CH, 128)
    mid = call(_middle, "middle", [
        ((SEGS - 2,) + table, bf16), ((SEGS - 2,) + target, f32), ((2, NQ, 8, 128), f32), ((2, EROWS, CH, 128), f32),
    ], [vmem] * 6, [hidden])(own, up, down, w1, bias, w2)
    return call(_refine, "refine", [((2, TR, TC), f32)], [vmem] * 12, [
        hidden, pltpu.VMEM((2,) + table, bf16), pltpu.VMEM((2,) + target, f32),
        *[pltpu.VMEM((2, NQ, 8, 128), f32) for _ in range(8)],
    ])(own, up, down, one, two, w1, bias, w2, *mid)[0]


def solution(mesh):
    return jax.shard_map(
        _local,
        mesh=mesh,
        in_specs=(P("row", "col"), P("row", "col"), P(None, "row", "col"), P(), P(), P()),
        out_specs=P(None, "row", "col"),
        check_vma=False,
    )
```

```python
import jax
import jax.numpy as jnp
from jax import lax
from jax.experimental import pallas as pl
from jax.experimental.pallas import tpu as pltpu
from jax.sharding import PartitionSpec as P

CH = 8
REACH = 16
ITERS = 3
STIFFNESS = 0.01
STEP = 0.5
EPS = 0.01

TR, TC = 32, 128
SIDE = 3
HALO_M = REACH + 1 + 2 + 2
HALO_PAD = 24
PADS = (HALO_PAD, 8, 8, 8)
TALL = TR + 2 * HALO_PAD
EROWS = 72
HROWS = 80
TOP = -(REACH + 3)
BLOCKS = EROWS // 8
FIXED_BLOCKS = range(2, 7)

SEGS = 5
WIDE = 26
NQ = 10
CUT = 20
PROWS = EROWS - CUT


FROM0 = REACH + 3
FAR = 117
PACE = 600
HALF = 5
AT4 = 62
FROM4 = WIDE * (SEGS - 1) - FROM0 - AT4


def _levels(span):
    out = []
    while span > 1:
        cut = (span + 1) // 2
        out.append(cut)
        span = cut
    return out


def _split(x):
    hi = x.astype(jnp.bfloat16)
    lo = (x - hi.astype(jnp.float32)).astype(jnp.bfloat16)
    return hi, lo


def _roll(x, shift, axis):
    size = x.shape[axis]
    shift = shift % size
    return x if shift == 0 else pltpu.roll(x, shift, axis)


def _pick(x, index):
    dims = lax.GatherDimensionNumbers(
        offset_dims=(), collapsed_slice_dims=(1,), start_index_map=(1,),
        operand_batching_dims=(0,), start_indices_batching_dims=(0,))
    return lax.gather(x, index[..., None], dims, (1, 1), mode=lax.GatherScatterMode.PROMISE_IN_BOUNDS)


def _dot(a, b):
    return jnp.dot(a, b, preferred_element_type=jnp.float32)


def _tall(own, one, two):
    r, n = lax.axis_index("row"), lax.axis_size("row")
    even = lax.rem(r, 2) == 0
    above = jnp.where(r > 0, jnp.where(even, two, one), 0.0)
    below = jnp.where(r < n - 1, jnp.where(even, one, two), 0.0)
    out, at = [], 0
    for x, pad in zip(own, PADS):
        out.append(jnp.concatenate([above[at:at + pad], x, below[at:at + pad]], axis=0))
        at += pad
    return out


def _fetch(pairs, sems):
    copies = [pltpu.make_async_copy(src, dst, sems.at[k]) for k, (src, dst) in enumerate(pairs)]
    for copy in copies:
        copy.start()
    for copy in copies:
        copy.wait()


def _own(own_ref):
    return [own_ref[TR * k:TR * k + TR] for k in range(4)]


def _pack_rows(mv_ref, fx_ref, fd_ref, one_ref, two_ref, own_ref, mv, fx, fd, sems):
    _fetch([(mv_ref, mv), (fx_ref, fx), (fd_ref, fd)], sems)
    even = lax.rem(lax.axis_index("row"), 2) == 0
    at = 0
    for k, x in enumerate([mv[...].astype(jnp.float32), fx[...].astype(jnp.float32), fd[0], fd[1]]):
        pad = PADS[k]
        own_ref[TR * k:TR * k + TR] = x
        first, last = x[:pad], x[TR - pad:]
        one_ref[at:at + pad] = jnp.where(even, last, first)
        two_ref[at:at + pad] = jnp.where(even, first, last)
        at += pad


def _weights(w1_ref, w2_ref, bias_ref, m1_ref, m2_ref, b_ref, w1, w2, flat, sems):
    _fetch([(w1_ref, w1), (w2_ref, w2)], sems)
    lane = lax.broadcasted_iota(jnp.int32, (CH, 128), 1)
    sub = lax.broadcasted_iota(jnp.int32, (CH, 128), 0)
    flat[0] = jnp.zeros((CH, 128), jnp.float32)
    flat[1] = jnp.zeros((CH, 128), jnp.float32)
    flat[0, :, 0:9] = w1[...]
    for c2 in range(CH):
        flat[1, :, 9 * c2:9 * c2 + 9] = w2[:, c2, :]
    b = jnp.zeros((CH, 128), jnp.float32)
    for c in range(CH):
        b = jnp.where(sub == c, bias_ref[c], b)
    b_ref[...] = b
    hi_rows, lo_rows = [], []
    for y in range(8):
        ky = lane % 16 - y - (HALO_PAD - HALO_M)
        v = _pick(flat[0], jnp.clip(3 * ky + lane // 16, 0, 127))
        v = jnp.where((ky >= 0) & (ky <= 2), v, 0.0)
        hi = v.astype(jnp.bfloat16).astype(jnp.float32)
        hi_rows.append(hi)
        lo_rows.append(v - hi)
    m1_ref[...] = jnp.concatenate(hi_rows + lo_rows, axis=0)[:, :48].astype(jnp.bfloat16)
    hi_rows, lo_rows = [], []
    for kx in range(3):
        for y in range(8):
            halves = []
            for half in range(2):
                at = lane + 128 * half
                at = jnp.where(at >= 80, at - 80, at)
                ky = at // 8 - y
                v = _pick(flat[1], jnp.clip(9 * (at % 8) + 3 * ky + kx, 0, 127))
                halves.append(jnp.where((ky >= 0) & (ky <= 2), v, 0.0))
            v = jnp.concatenate(halves, axis=1)
            hi = v.astype(jnp.bfloat16).astype(jnp.float32)
            wide = lax.broadcasted_iota(jnp.int32, (CH, 256), 1)
            hi_rows.append(hi)
            lo_rows.append(jnp.where(wide < 80, v - hi, 0.0))
    m2_ref[...] = jnp.concatenate(hi_rows + lo_rows, axis=0)[:, :160].astype(jnp.bfloat16)


def _pack_cols(own_ref, up_ref, down_ref, _, one_ref, two_ref):
    even = lax.rem(lax.axis_index("col"), 2) == 0
    tall = _tall(_own(own_ref), up_ref[...], down_ref[...])
    lane = lax.broadcasted_iota(jnp.int32, (8, 128), 1)
    for i in range(TALL // 8):
        first = last = None
        for k in (3, 2, 1, 0):
            if 8 * i < tall[k].shape[0]:
                v = tall[k][8 * i:8 * i + 8]
                a, b = _roll(v, 32 * k, 1), _roll(v, 32 * k + HALO_M, 1)
                first = a if first is None else jnp.where(lane < 32 * k + 32, a, first)
                last = b if last is None else jnp.where(lane < 32 * k + 32, b, last)
        one_ref[8 * i:8 * i + 8] = jnp.where(even, last, first)
        two_ref[8 * i:8 * i + 8] = jnp.where(even, first, last)


def _edges(own, up, down, one, two):
    c, n = lax.axis_index("col"), lax.axis_size("col")
    even = lax.rem(c, 2) == 0
    left = jnp.where(c > 0, jnp.where(even, two, one), 0.0)
    right = jnp.where(c < n - 1, jnp.where(even, one, two), 0.0)
    tall = _tall(own, up, down)
    images = []
    for k, x in enumerate(tall[:2]):
        lane = lax.broadcasted_iota(jnp.int32, x.shape, 1) - 64 * k
        r = x.shape[0]
        v = jnp.where(lane < 32 + TC - FAR, _roll(x, 64 * k + 32 - FAR, 1), _roll(right[:r], 32 * k + 32 + TC - FAR, 1))
        v = jnp.where(lane < 32, _roll(x, 64 * k + HALO_M, 1), v)
        images.append(jnp.where(lane < HALO_M, _roll(left[:r], 32 * k, 1), v))
    blank = jnp.zeros((16, 128), jnp.float32)
    fixed = jnp.concatenate([blank, images[1], blank], axis=0)
    lane = lax.broadcasted_iota(jnp.int32, fixed.shape, 1)
    out = [jnp.where(lane < 64, images[0], fixed)]
    for k in (2, 3):
        x = tall[k]
        lane = lax.broadcasted_iota(jnp.int32, x.shape, 1)
        r = x.shape[0]
        v = jnp.where(lane < TC - FROM4, _roll(x, -FROM4, 1), _roll(right[:r], TC - FROM4 - 32 * k, 1))
        v = jnp.where(lane < AT4, _roll(x, FROM0, 1), v)
        out.append(jnp.where(lane < FROM0, _roll(left[:r], FROM0 - HALO_M - 32 * k, 1), v))
    return out


class _Place:
    def __init__(self):
        self.row, self.col = TR * lax.axis_index("row"), TC * lax.axis_index("col")
        self.rows, self.cols = TR * lax.axis_size("row"), TC * lax.axis_size("col")

    def keep(self, y, col_ok):
        r = self.row + y
        ok = jnp.where((r >= 0) & (r < self.rows), 1, 0)
        return jnp.where(col_ok, ok.astype(jnp.float32), 0.0)


def _embed(place, images, column, tops, blocks, w1_ref, bias_ref, w2_ref, hs, sink):
    bias = bias_ref[...]
    x = place.col + column
    col_ok = (x >= 0) & (x < place.cols)
    shifted = [jnp.concatenate([_roll(v, 1 - kx, 1) for v in images], axis=1) for kx in range(3)]
    count = max(max(b) for b in blocks) + 1
    for b in range(count + 1):
        if 8 * b + 16 > shifted[0].shape[0]:
            hs[:, 64 * b:64 * b + 64, :] = jnp.zeros((2, 64, 256), jnp.bfloat16)
            continue
        t = _dot(w1_ref[...], jnp.concatenate([v[8 * b:8 * b + 16] for v in shifted], axis=0).astype(jnp.bfloat16))
        pre = t[:64] + t[64:]
        for h in range(2):
            at = slice(128 * h, 128 * h + 128)
            if b not in blocks[h] and b - 1 not in blocks[h]:
                hs[:, 64 * b:64 * b + 64, at] = jnp.zeros((2, 64, 128), jnp.bfloat16)
                continue
            v = jnp.concatenate([
                jnp.maximum(pre[CH * k:CH * k + CH, at] + bias, 0.0) * place.keep(tops[h] - 1 + 8 * b + k, col_ok)
                for k in range(8)], axis=0)
            hs[0, 64 * b:64 * b + 64, at], hs[1, 64 * b:64 * b + 64, at] = _split(v)
        yield 200
    for b in range(count):
        t = _dot(w2_ref[...], jnp.concatenate([hs[0, 64 * b:64 * b + 80], hs[1, 64 * b:64 * b + 80]], axis=0))
        v = t[:192] + t[192:]
        for h in range(2):
            if b not in blocks[h]:
                continue
            o = [v[64 * kx:64 * kx + 64, 128 * h:128 * h + 128] for kx in range(3)]
            e = o[1] + _roll(o[0], 1, 1) + _roll(o[2], -1, 1)
            sink(b, h, [e[CH * k:CH * k + CH] * place.keep(tops[h] + 8 * b + k, col_ok) for k in range(8)])
        yield 250


def _build(moving, fixed, window, pixel, e3, ef):
    lane = lax.broadcasted_iota(jnp.int32, (8, 128), 1)
    for r in range(0, PROWS, 2):
        out = []
        for k in (r, r + 1):
            e0 = jnp.where(lane < 64, _roll(moving[k], -window, 1), _roll(moving[k + CUT], 64 - window, 1))
            left, right = _roll(e0, 1, 1), _roll(e0, -1, 1)
            p1 = 0.5 * (right - left)
            p2 = 0.5 * (right + left) - e0
            out += [e0 + 0.25 * p2, p1, p2]
        hi, lo = _split(jnp.concatenate(out, axis=0))
        e3[24 * r:24 * r + 48, 0:128] = hi
        e3[24 * r:24 * r + 48, 128:256] = lo
        yield 25
    for q in range(NQ):
        cur = None
        for i in range(4):
            row = min(max(4 * q - 4 + i, -2), TR + 1) - TOP
            v = _roll(fixed[row], 32 * i - pixel, 1)
            cur = v if i == 0 else jnp.where(lane < 32 * i, cur, v)
        ef[q] = cur
        yield 25


def _start(field, pixel, s, raw):
    lane = lax.broadcasted_iota(jnp.int32, (8, 128), 1)
    sub = lax.broadcasted_iota(jnp.int32, (8, 128), 0)
    mine = lane // 32 == sub % 4
    for comp in range(2):
        for b in range(NQ // 2):
            v = field[comp][8 * b + 4:8 * b + 12]
            v = _pick(v, (lane - 32 * (sub % 4) + pixel) & 127)
            for k in range(2):
                raw[comp, 2 * b + k, s:s + 1, :] = jnp.sum(
                    jnp.where(mine & (sub // 4 == k), v, 0.0), axis=0, keepdims=True)


def _middle(own_ref, up_ref, down_ref, w1_ref, bias_ref, w2_ref, e3_ref, ef_ref, raw_ref, rows_ref, hs):
    moving, fixed, *field = _tall(_own(own_ref), up_ref[...], down_ref[...])
    lane = lax.broadcasted_iota(jnp.int32, (CH, 128), 1)
    rows = [{}, {}]

    def sink(b, h, got):
        for k, v in enumerate(got):
            rows[h][8 * b + k] = v
            rows_ref[h, 8 * b + k] = v

    blank = jnp.zeros((16, 128), jnp.float32)
    fixed = jnp.concatenate([blank, fixed, blank], axis=0)
    for _ in _embed(_Place(), [moving, fixed], lane, [TOP, TOP], [range(BLOCKS), FIXED_BLOCKS],
                    w1_ref, bias_ref, w2_ref, hs, sink):
        pass
    raw_ref[...] = jnp.zeros_like(raw_ref)
    for s in range(1, SEGS - 1):
        _start(field, WIDE * s - SIDE, s, raw_ref)
        for _ in _build(rows[0], rows[1], WIDE * s - 3 - REACH, WIDE * s - SIDE, e3_ref.at[s - 1], ef_ref.at[s - 1]):
            pass


def _refine(own_ref, up_ref, down_ref, one_ref, two_ref, w1_ref, bias_ref, w2_ref, mid3_ref, midf_ref, midr_ref, rows_ref,
            out_ref, hs, e3, ef, raw, m1, m2, sq, disp, frac, idx, dat):
    place = _Place()
    row0, col0, rows, cols = place.row, place.col, place.rows, place.cols
    lane = lax.broadcasted_iota(jnp.int32, (8, 128), 1)
    sub = lax.broadcasted_iota(jnp.int32, (8, 128), 0)
    image, *field = _edges(_own(own_ref), up_ref[...], down_ref[...], one_ref[...], two_ref[...])
    raw[...] = midr_ref[...]
    _start(field, REACH, 0, raw)
    _start(field, AT4 + REACH, SEGS - 1, raw)
    tables = [e3.at[0]] + [mid3_ref.at[k] for k in range(SEGS - 2)] + [e3.at[1]]
    targets = [ef.at[0]] + [midf_ref.at[k] for k in range(SEGS - 2)] + [ef.at[1]]

    def edges(ready):
        rows = [[{}, {}], [{}, {}]]

        def sink(b, h, got):
            for k, v in enumerate(got):
                r = 8 * (b + HALF * h) + k
                mine = rows_ref[0, r]
                rows[0][0][r] = jnp.where(lane < FROM0 + 2, _roll(v, FROM0 - HALO_M, 1), _roll(mine, FROM0, 1))
                rows[1][0][r] = jnp.where(lane < TC - FROM4 - 2, _roll(mine, -FROM4, 1), _roll(v, FAR - 32 - FROM4, 1))
                if r // 8 in FIXED_BLOCKS:
                    mine = rows_ref[1, r]
                    rows[0][1][r] = jnp.where(lane < FROM0 + 2, _roll(v, FROM0 - HALO_M - 64, 1), _roll(mine, FROM0, 1))
                    rows[1][1][r] = jnp.where(lane < TC - FROM4 - 2, _roll(mine, -FROM4, 1), _roll(v, FAR - 96 - FROM4, 1))

        column = jnp.where(lane % 64 < 32, lane % 32 - HALO_M, lane % 32 + FAR)
        blank = jnp.zeros((8, 128), jnp.float32)
        halves = [image[:8 * HALF + 16], jnp.concatenate([image[8 * HALF:], blank, blank], axis=0)]
        yield from _embed(place, halves, column, [TOP, TOP + 8 * HALF], [range(HALF), range(BLOCKS - HALF)],
                          w1_ref, bias_ref, w2_ref, hs, sink)
        yield from _build(rows[0][0], rows[0][1], 0, REACH, e3.at[0], ef.at[0])
        ready.extend((q0, 0) for q0 in range(0, NQ, 2))
        yield from _build(rows[1][0], rows[1][1], AT4, AT4 + REACH, e3.at[1], ef.at[1])
        ready.extend((q0, SEGS - 1) for q0 in range(0, NQ, 2))

    m1[...] = jnp.zeros_like(m1)
    m2[...] = jnp.zeros_like(m2)
    dat[...] = jnp.zeros_like(dat)

    j = lane % 32
    x = col0 + WIDE * sub - SIDE + j
    col_in = (x >= 0) & (x < cols)
    iota_k = lax.broadcasted_iota(jnp.int32, (128, 256), 0).astype(jnp.float32).astype(jnp.bfloat16)

    def group(q0, s):
        start = max(4 * q0 - 4, -2) + 2

        def pair(ref, comp, count):
            return jnp.concatenate(
                [jnp.broadcast_to(ref[comp, q0 + k, s:s + 1, :], (count, 128)) for k in range(2)], axis=1)

        col = pair(idx, 1, 1) + jnp.where(pair(idx, 0, 1) >= start + CUT, 64.0, 0.0)
        pick = jnp.where(iota_k == jnp.broadcast_to(col.astype(jnp.bfloat16), (128, 256)),
                         jnp.bfloat16(1.0), jnp.bfloat16(0.0))
        count = CUT + 2
        t = _dot(tables[s][24 * start:24 * (start + count), :], jnp.concatenate([pick, pick], axis=0))
        base = pair(idx, 0, 8) - (start * 1.0)
        base = jnp.where(base >= CUT, base - CUT, base)
        conds = []
        for cut in _levels(CUT):
            c = base >= cut
            conds.append((cut, c))
            base = jnp.where(c, base - cut, base)
        taps = []
        for b in range(3):
            T = [t[24 * k + 8 * b:24 * k + 8 * b + 8] for k in range(count)]
            for cut, c in conds:
                T = [jnp.where(c, T[k + cut], T[k]) if k + cut < len(T) else T[k] for k in range(cut + 2)]
            taps.append(T)
        fr, fc = pair(frac, 0, 8), pair(frac, 1, 8)
        A, B = [], []
        for a in range(3):
            w = fc * taps[2][a]
            v = taps[1][a] + w
            A.append(taps[0][a] + fc * v)
            B.append(v + w)
        da, qa = 0.5 * (A[2] - A[0]), 0.5 * (A[2] + A[0]) - A[1]
        db, qb = 0.5 * (B[2] - B[0]), 0.5 * (B[2] + B[0]) - B[1]
        wa = fr * qa
        va = da + wa
        warped = A[1] + 0.25 * qa + fr * va
        slope_row = va + wa
        slope_col = B[1] + 0.25 * qb + fr * (db + fr * qb)
        target = jnp.concatenate([targets[s][q0], targets[s][q0 + 1]], axis=1)
        miss = (warped - target) * (2.0 / CH)
        for comp, slope in ((0, slope_row), (1, slope_col)):
            total = jnp.sum(miss * slope, axis=0, keepdims=True)
            for k in range(2):
                dat[comp, q0 + k, s:s + 1, :] = total[:, 128 * k:128 * k + 128]

    def step(t):
        for q in range(NQ):
            y = 4 * q - 4 + lane // 32
            ok = col_in & (row0 + y >= 0) & (row0 + y < rows)
            for comp, origin in ((0, y + REACH + 2), (1, j + REACH)):
                v = jnp.tanh(raw[comp, q] * (1.0 / REACH))
                d = REACH * v
                n = jnp.floor(d + 0.5)
                sq[comp, q] = v
                disp[comp, q] = jnp.where(ok, d, 0.0)
                frac[comp, q] = d - n
                idx[comp, q] = n + origin.astype(jnp.float32)
        if t == 0:
            ready, spent = [(q0, s) for s in range(1, SEGS - 1) for q0 in range(0, NQ, 2)], 0
            for length in edges(ready):
                spent += length
                while spent >= PACE and ready:
                    spent -= PACE
                    group(*ready.pop(0))
        else:
            ready = [(q0, s) for q0 in (range(0, NQ, 2) if t < 2 else range(1, NQ - 1, 2)) for s in range(SEGS)]
        for at in ready:
            group(*at)
        one, two = 1.0 / (1.0 - 0.9 ** (t + 1)), 1.0 / (1.0 - 0.999 ** (t + 1))
        for comp in range(2):
            for q in range(NQ) if t < 2 else range(1, NQ - 1):
                d = disp[comp, q]
                up = jnp.where(lane < 96, _roll(d, -32, 1), _roll(disp[comp, min(q + 1, NQ - 1)], -32, 1))
                down = jnp.where(lane >= 32, _roll(d, 32, 1), _roll(disp[comp, max(q - 1, 0)], 32, 1))
                around = up + down + _roll(d, 1, 1) + _roll(d, -1, 1)
                v = sq[comp, q]
                grad = (dat[comp, q] + 2.0 * STIFFNESS * (4.0 * REACH * v - around)) * (1.0 - v * v)
                a = 0.9 * m1[comp, q] + 0.1 * grad
                b = 0.999 * m2[comp, q] + 0.001 * grad * grad
                m1[comp, q] = a
                m2[comp, q] = b
                raw[comp, q] = raw[comp, q] - STEP * (a * one) / (jnp.sqrt(b * two) + EPS)

    for t in range(ITERS):
        step(t)

    own = _own(own_ref)
    for comp in range(2):
        for b in range(TR // 8):
            out = None
            for s in range(SEGS):
                v = jnp.where(sub < 4, jnp.broadcast_to(raw[comp, 2 * b + 1, s:s + 1, :], (8, 128)),
                              jnp.broadcast_to(raw[comp, 2 * b + 2, s:s + 1, :], (8, 128)))
                v = _pick(v, (lane + 32 * (sub % 4) + (128 + SIDE - WIDE * s)) & 127)
                out = v if s == 0 else jnp.where(lane < WIDE * s, out, v)
            out_ref[comp, 8 * b:8 * b + 8] = out - own[2 + comp][8 * b:8 * b + 8]


def _swaps(n, first, wrap):
    return [p for a in range(first, n if wrap else n - 1, 2) for p in ((a, (a + 1) % n), ((a + 1) % n, a))]


def _exchange(pair, axis):
    n = lax.axis_size(axis)
    return [lax.ppermute(x, axis, _swaps(n, k, axis == "row")) for k, x in enumerate(pair)]


def _local(fixed_section, moving_section, field_init, first_weight, first_bias, second_weight):
    vmem = pl.BlockSpec(memory_space=pltpu.VMEM)
    smem = pl.BlockSpec(memory_space=pltpu.SMEM)
    anywhere = pl.BlockSpec(memory_space=pltpu.HBM)
    f32, bf16 = jnp.float32, jnp.bfloat16

    def call(body, name, out, specs, scratch):
        return pl.pallas_call(
            body,
            out_shape=[jax.ShapeDtypeStruct(*x) for x in out],
            in_specs=specs,
            out_specs=[vmem] * len(out),
            scratch_shapes=scratch,
            compiler_params=pltpu.CompilerParams(vmem_limit_bytes=48 * 2 ** 20),
            name=name,
        )

    strip = ((sum(PADS), 128), f32)
    one, two, own = call(_pack_rows, "pack_rows", [strip, strip, ((4 * TR, TC), f32)], [anywhere] * 3, [
        pltpu.VMEM((TR, TC), bf16), pltpu.VMEM((TR, TC), bf16), pltpu.VMEM((2, TR, TC), f32),
        pltpu.SemaphoreType.DMA((3,))])(*[pltpu.with_memory_space_constraint(x, pltpu.HBM) for x in (moving_section, fixed_section, field_init)])
    up, down = _exchange((one, two), "row")
    w1, w2, bias = call(_weights, "weights", [((128, 48), bf16), ((384, 160), bf16), ((CH, 128), f32)],
                        [anywhere, anywhere, smem], [
        pltpu.VMEM((CH, 9), f32), pltpu.VMEM((CH, CH, 9), f32), pltpu.VMEM((2, CH, 128), f32),
        pltpu.SemaphoreType.DMA((2,))])(*[pltpu.with_memory_space_constraint(x, pltpu.HBM) for x in (first_weight, second_weight)], first_bias)
    strip = ((TALL, 128), f32)
    one, two = _exchange(call(_pack_cols, "pack_cols", [strip, strip], [vmem] * 4, [])(own, up, down, bias), "col")
    hidden = pltpu.VMEM((2, HROWS * CH, 256), bf16)
    table, target = (PROWS * 24, 256), (NQ, CH, 128)
    mid = call(_middle, "middle", [
        ((SEGS - 2,) + table, bf16), ((SEGS - 2,) + target, f32), ((2, NQ, 8, 128), f32), ((2, EROWS, CH, 128), f32),
    ], [vmem] * 6, [hidden])(own, up, down, w1, bias, w2)
    return call(_refine, "refine", [((2, TR, TC), f32)], [vmem] * 12, [
        hidden, pltpu.VMEM((2,) + table, bf16), pltpu.VMEM((2,) + target, f32),
        *[pltpu.VMEM((2, NQ, 8, 128), f32) for _ in range(8)],
    ])(own, up, down, one, two, w1, bias, w2, *mid)[0]


def solution(mesh):
    return jax.shard_map(
        _local,
        mesh=mesh,
        in_specs=(P("row", "col"), P("row", "col"), P(None, "row", "col"), P(), P(), P()),
        out_specs=P(None, "row", "col"),
        check_vma=False,
    )
```

```python
import jax
import jax.numpy as jnp
from jax import lax
from jax.experimental import pallas as pl
from jax.experimental.pallas import tpu as pltpu
from jax.sharding import PartitionSpec as P

CH = 8
REACH = 16
ITERS = 3
STIFFNESS = 0.01
STEP = 0.5
EPS = 0.01

TR, TC = 32, 128
SIDE = 3
HALO_M = REACH + 1 + 2 + 2
HALO_PAD = 24
PADS = (HALO_PAD, 8, 8, 8)
TALL = TR + 2 * HALO_PAD
WIDTHS = (HALO_M, 4, SIDE, SIDE)
STRIPS = (0, HALO_M, HALO_M + 4, HALO_M + 4 + SIDE)
EROWS = 72
HROWS = 80
TOP = -(REACH + 3)
BLOCKS = EROWS // 8
FIXED_BLOCKS = range(2, 7)

SEGS = 5
WIDE = 26
NQ = 10
CUT = 20
PROWS = EROWS - CUT


FROM0 = REACH + 3
FAR = 117
PACE = 300
HALF = 5
AT4 = 62
FROM4 = WIDE * (SEGS - 1) - FROM0 - AT4


def _levels(span):
    out = []
    while span > 1:
        cut = (span + 1) // 2
        out.append(cut)
        span = cut
    return out


def _split(x):
    hi = x.astype(jnp.bfloat16)
    lo = (x - hi.astype(jnp.float32)).astype(jnp.bfloat16)
    return hi, lo


def _roll(x, shift, axis):
    size = x.shape[axis]
    shift = shift % size
    return x if shift == 0 else pltpu.roll(x, shift, axis)


def _pick(x, index):
    dims = lax.GatherDimensionNumbers(
        offset_dims=(), collapsed_slice_dims=(1,), start_index_map=(1,),
        operand_batching_dims=(0,), start_indices_batching_dims=(0,))
    return lax.gather(x, index[..., None], dims, (1, 1), mode=lax.GatherScatterMode.PROMISE_IN_BOUNDS)


def _dot(a, b):
    return jnp.dot(a, b, preferred_element_type=jnp.float32)


def _tall(own, one, two):
    r, n = lax.axis_index("row"), lax.axis_size("row")
    even = lax.rem(r, 2) == 0
    above = jnp.where(r > 0, jnp.where(even, two, one), 0.0)
    below = jnp.where(r < n - 1, jnp.where(even, one, two), 0.0)
    out, at = [], 0
    for x, pad in zip(own, PADS):
        out.append(jnp.concatenate([above[at:at + pad], x, below[at:at + pad]], axis=0))
        at += pad
    return out


def _fetch(pairs, sems):
    copies = [pltpu.make_async_copy(src, dst, sems.at[k]) for k, (src, dst) in enumerate(pairs)]
    for copy in copies:
        copy.start()
    for copy in copies:
        copy.wait()


def _own(own_ref):
    return [own_ref[TR * k:TR * k + TR] for k in range(4)]


def _pack_rows(mv_ref, fx_ref, fd_ref, one_ref, two_ref, own_ref, mv, fx, fd, sems):
    _fetch([(mv_ref, mv), (fx_ref, fx), (fd_ref, fd)], sems)
    even = lax.rem(lax.axis_index("row"), 2) == 0
    at = 0
    for k, x in enumerate([mv[...].astype(jnp.float32), fx[...].astype(jnp.float32), fd[0], fd[1]]):
        pad = PADS[k]
        own_ref[TR * k:TR * k + TR] = x
        first, last = x[:pad], x[TR - pad:]
        one_ref[at:at + pad] = jnp.where(even, last, first)
        two_ref[at:at + pad] = jnp.where(even, first, last)
        at += pad


def _weights(w1_ref, w2_ref, bias_ref, m1_ref, m2_ref, b_ref, w1, w2, flat, sems):
    _fetch([(w1_ref, w1), (w2_ref, w2)], sems)
    lane = lax.broadcasted_iota(jnp.int32, (CH, 128), 1)
    sub = lax.broadcasted_iota(jnp.int32, (CH, 128), 0)
    flat[0] = jnp.zeros((CH, 128), jnp.float32)
    flat[1] = jnp.zeros((CH, 128), jnp.float32)
    flat[0, :, 0:9] = w1[...]
    for c2 in range(CH):
        flat[1, :, 9 * c2:9 * c2 + 9] = w2[:, c2, :]
    b = jnp.zeros((CH, 128), jnp.float32)
    for c in range(CH):
        b = jnp.where(sub == c, bias_ref[c], b)
    b_ref[...] = b
    hi_rows, lo_rows = [], []
    for y in range(8):
        ky = lane % 16 - y - (HALO_PAD - HALO_M)
        v = _pick(flat[0], jnp.clip(3 * ky + lane // 16, 0, 127))
        v = jnp.where((ky >= 0) & (ky <= 2), v, 0.0)
        hi = v.astype(jnp.bfloat16).astype(jnp.float32)
        hi_rows.append(hi)
        lo_rows.append(v - hi)
    m1_ref[...] = jnp.concatenate(hi_rows + lo_rows, axis=0)[:, :48].astype(jnp.bfloat16)
    hi_rows, lo_rows = [], []
    for kx in range(3):
        for y in range(8):
            halves = []
            for half in range(2):
                at = lane + 128 * half
                at = jnp.where(at >= 80, at - 80, at)
                ky = at // 8 - y
                v = _pick(flat[1], jnp.clip(9 * (at % 8) + 3 * ky + kx, 0, 127))
                halves.append(jnp.where((ky >= 0) & (ky <= 2), v, 0.0))
            v = jnp.concatenate(halves, axis=1)
            hi = v.astype(jnp.bfloat16).astype(jnp.float32)
            wide = lax.broadcasted_iota(jnp.int32, (CH, 256), 1)
            hi_rows.append(hi)
            lo_rows.append(jnp.where(wide < 80, v - hi, 0.0))
    m2_ref[...] = jnp.concatenate(hi_rows + lo_rows, axis=0)[:, :160].astype(jnp.bfloat16)


def _pack_cols(own_ref, up_ref, down_ref, _, one_ref, two_ref):
    even = lax.rem(lax.axis_index("col"), 2) == 0
    tall = _tall(_own(own_ref), up_ref[...], down_ref[...])
    lane = lax.broadcasted_iota(jnp.int32, (8, 128), 1)
    for i in range(0, TALL // 8, 4):
        first = last = jnp.zeros((8, 128), jnp.float32)
        for b in range(i, min(i + 4, TALL // 8)):
            for k, x in enumerate(tall):
                if 8 * b < x.shape[0]:
                    v, at = x[8 * b:8 * b + 8], 32 * (b - i) + STRIPS[k]
                    first = jnp.where(lane < at, first, _roll(v, at, 1))
                    last = jnp.where(lane < at, last, _roll(v, at + WIDTHS[k], 1))
        one_ref[2 * i:2 * i + 8] = jnp.where(even, last, first)
        two_ref[2 * i:2 * i + 8] = jnp.where(even, first, last)


def _unpack(x):
    return jnp.concatenate([_roll(x[8 * (b // 4):8 * (b // 4) + 8], -32 * (b % 4), 1) for b in range(TALL // 8)], axis=0)


def _edges(own, up, down, one, two):
    c, n = lax.axis_index("col"), lax.axis_size("col")
    even = lax.rem(c, 2) == 0
    left = _unpack(jnp.where(c > 0, jnp.where(even, two, one), 0.0))
    right = _unpack(jnp.where(c < n - 1, jnp.where(even, one, two), 0.0))
    tall = _tall(own, up, down)
    images = []
    for k, x in enumerate(tall[:2]):
        lane = lax.broadcasted_iota(jnp.int32, x.shape, 1) - 64 * k
        r = x.shape[0]
        v = jnp.where(lane < 32 + TC - FAR, _roll(x, 64 * k + 32 - FAR, 1), _roll(right[:r], 64 * k + 32 + TC - FAR - STRIPS[k], 1))
        v = jnp.where(lane < 32, _roll(x, 64 * k + HALO_M, 1), v)
        images.append(jnp.where(lane < HALO_M, _roll(left[:r], 64 * k + HALO_M - WIDTHS[k] - STRIPS[k], 1), v))
    blank = jnp.zeros((16, 128), jnp.float32)
    fixed = jnp.concatenate([blank, images[1], blank], axis=0)
    lane = lax.broadcasted_iota(jnp.int32, fixed.shape, 1)
    out = [jnp.where(lane < 64, images[0], fixed)]
    for k in (2, 3):
        x = tall[k]
        lane = lax.broadcasted_iota(jnp.int32, x.shape, 1)
        r = x.shape[0]
        v = jnp.where(lane < TC - FROM4, _roll(x, -FROM4, 1), _roll(right[:r], TC - FROM4 - STRIPS[k], 1))
        v = jnp.where(lane < AT4, _roll(x, FROM0, 1), v)
        out.append(jnp.where(lane < FROM0, _roll(left[:r], FROM0 - WIDTHS[k] - STRIPS[k], 1), v))
    return out


class _Place:
    def __init__(self):
        self.row, self.col = TR * lax.axis_index("row"), TC * lax.axis_index("col")
        self.rows, self.cols = TR * lax.axis_size("row"), TC * lax.axis_size("col")

    def keep(self, y, col_ok):
        r = self.row + y
        ok = jnp.where((r >= 0) & (r < self.rows), 1, 0)
        return jnp.where(col_ok, ok.astype(jnp.float32), 0.0)


def _embed(place, images, column, tops, blocks, w1_ref, bias_ref, w2_ref, hs, sink):
    bias = bias_ref[...]
    x = place.col + column
    col_ok = (x >= 0) & (x < place.cols)
    shifted = [jnp.concatenate([_roll(v, 1 - kx, 1) for v in images], axis=1) for kx in range(3)]
    count = max(max(b) for b in blocks) + 1
    for b in range(count + 1):
        if 8 * b + 16 > shifted[0].shape[0]:
            hs[:, 64 * b:64 * b + 64, :] = jnp.zeros((2, 64, 256), jnp.bfloat16)
            continue
        t = _dot(w1_ref[...], jnp.concatenate([v[8 * b:8 * b + 16] for v in shifted], axis=0).astype(jnp.bfloat16))
        pre = t[:64] + t[64:]
        for h in range(2):
            at = slice(128 * h, 128 * h + 128)
            if b not in blocks[h] and b - 1 not in blocks[h]:
                hs[:, 64 * b:64 * b + 64, at] = jnp.zeros((2, 64, 128), jnp.bfloat16)
                continue
            v = jnp.concatenate([
                jnp.maximum(pre[CH * k:CH * k + CH, at] + bias, 0.0) * place.keep(tops[h] - 1 + 8 * b + k, col_ok)
                for k in range(8)], axis=0)
            hs[0, 64 * b:64 * b + 64, at], hs[1, 64 * b:64 * b + 64, at] = _split(v)
        yield 100
    for b in range(count):
        t = _dot(w2_ref[...], jnp.concatenate([hs[0, 64 * b:64 * b + 80], hs[1, 64 * b:64 * b + 80]], axis=0))
        v = t[:192] + t[192:]
        for h in range(2):
            if b not in blocks[h]:
                continue
            o = [v[64 * kx:64 * kx + 64, 128 * h:128 * h + 128] for kx in range(3)]
            e = o[1] + _roll(o[0], 1, 1) + _roll(o[2], -1, 1)
            sink(b, h, [e[CH * k:CH * k + CH] * place.keep(tops[h] + 8 * b + k, col_ok) for k in range(8)])
        yield 120


def _build(moving, fixed, window, pixel, e3, ef):
    lane = lax.broadcasted_iota(jnp.int32, (8, 128), 1)
    for r in range(0, PROWS, 2):
        out = []
        for k in (r, r + 1):
            e0 = jnp.where(lane < 64, _roll(moving[k], -window, 1), _roll(moving[k + CUT], 64 - window, 1))
            left, right = _roll(e0, 1, 1), _roll(e0, -1, 1)
            p1 = 0.5 * (right - left)
            p2 = 0.5 * (right + left) - e0
            out += [e0 + 0.25 * p2, p1, p2]
        hi, lo = _split(jnp.concatenate(out, axis=0))
        e3[24 * r:24 * r + 48, 0:128] = hi
        e3[24 * r:24 * r + 48, 128:256] = lo
        yield 25
    for q in range(NQ):
        cur = None
        for i in range(4):
            row = min(max(4 * q - 4 + i, -2), TR + 1) - TOP
            v = _roll(fixed[row], 32 * i - pixel, 1)
            cur = v if i == 0 else jnp.where(lane < 32 * i, cur, v)
        ef[q] = cur
        yield 25


def _start(field, pixel, s, raw):
    lane = lax.broadcasted_iota(jnp.int32, (8, 128), 1)
    sub = lax.broadcasted_iota(jnp.int32, (8, 128), 0)
    mine = lane // 32 == sub % 4
    for comp in range(2):
        for b in range(NQ // 2):
            v = field[comp][8 * b + 4:8 * b + 12]
            v = _pick(v, (lane - 32 * (sub % 4) + pixel) & 127)
            for k in range(2):
                raw[comp, 2 * b + k, s:s + 1, :] = jnp.sum(
                    jnp.where(mine & (sub // 4 == k), v, 0.0), axis=0, keepdims=True)


def _middle(own_ref, up_ref, down_ref, w1_ref, bias_ref, w2_ref, e3_ref, ef_ref, raw_ref, rows_ref, hs):
    moving, fixed, *field = _tall(_own(own_ref), up_ref[...], down_ref[...])
    lane = lax.broadcasted_iota(jnp.int32, (CH, 128), 1)
    rows = [{}, {}]

    def sink(b, h, got):
        for k, v in enumerate(got):
            rows[h][8 * b + k] = v
            rows_ref[h, 8 * b + k] = v

    blank = jnp.zeros((16, 128), jnp.float32)
    fixed = jnp.concatenate([blank, fixed, blank], axis=0)
    for _ in _embed(_Place(), [moving, fixed], lane, [TOP, TOP], [range(BLOCKS), FIXED_BLOCKS],
                    w1_ref, bias_ref, w2_ref, hs, sink):
        pass
    raw_ref[...] = jnp.zeros_like(raw_ref)
    for s in range(1, SEGS - 1):
        _start(field, WIDE * s - SIDE, s, raw_ref)
        for _ in _build(rows[0], rows[1], WIDE * s - 3 - REACH, WIDE * s - SIDE, e3_ref.at[s - 1], ef_ref.at[s - 1]):
            pass


def _refine(own_ref, up_ref, down_ref, one_ref, two_ref, w1_ref, bias_ref, w2_ref, mid3_ref, midf_ref, midr_ref, rows_ref,
            out_ref, hs, e3, ef, raw, m1, m2, sq, disp, frac, idx, dat):
    place = _Place()
    row0, col0, rows, cols = place.row, place.col, place.rows, place.cols
    lane = lax.broadcasted_iota(jnp.int32, (8, 128), 1)
    sub = lax.broadcasted_iota(jnp.int32, (8, 128), 0)
    image, *field = _edges(_own(own_ref), up_ref[...], down_ref[...], one_ref[...], two_ref[...])
    raw[...] = midr_ref[...]
    _start(field, REACH, 0, raw)
    _start(field, AT4 + REACH, SEGS - 1, raw)
    tables = [e3.at[0]] + [mid3_ref.at[k] for k in range(SEGS - 2)] + [e3.at[1]]
    targets = [ef.at[0]] + [midf_ref.at[k] for k in range(SEGS - 2)] + [ef.at[1]]

    def edges(ready):
        rows = [[{}, {}], [{}, {}]]

        def sink(b, h, got):
            for k, v in enumerate(got):
                r = 8 * (b + HALF * h) + k
                mine = rows_ref[0, r]
                rows[0][0][r] = jnp.where(lane < FROM0 + 2, _roll(v, FROM0 - HALO_M, 1), _roll(mine, FROM0, 1))
                rows[1][0][r] = jnp.where(lane < TC - FROM4 - 2, _roll(mine, -FROM4, 1), _roll(v, FAR - 32 - FROM4, 1))
                if r // 8 in FIXED_BLOCKS:
                    mine = rows_ref[1, r]
                    rows[0][1][r] = jnp.where(lane < FROM0 + 2, _roll(v, FROM0 - HALO_M - 64, 1), _roll(mine, FROM0, 1))
                    rows[1][1][r] = jnp.where(lane < TC - FROM4 - 2, _roll(mine, -FROM4, 1), _roll(v, FAR - 96 - FROM4, 1))

        column = jnp.where(lane % 64 < 32, lane % 32 - HALO_M, lane % 32 + FAR)
        blank = jnp.zeros((8, 128), jnp.float32)
        halves = [image[:8 * HALF + 16], jnp.concatenate([image[8 * HALF:], blank, blank], axis=0)]
        yield from _embed(place, halves, column, [TOP, TOP + 8 * HALF], [range(HALF), range(BLOCKS - HALF)],
                          w1_ref, bias_ref, w2_ref, hs, sink)
        yield from _build(rows[0][0], rows[0][1], 0, REACH, e3.at[0], ef.at[0])
        ready.extend((q0, 0) for q0 in range(0, NQ, 2))
        yield from _build(rows[1][0], rows[1][1], AT4, AT4 + REACH, e3.at[1], ef.at[1])
        ready.extend((q0, SEGS - 1) for q0 in range(0, NQ, 2))

    dat[...] = jnp.zeros_like(dat)

    j = lane % 32
    x = col0 + WIDE * sub - SIDE + j
    col_in = (x >= 0) & (x < cols)
    iota_k = lax.broadcasted_iota(jnp.int32, (128, 256), 0).astype(jnp.float32).astype(jnp.bfloat16)

    def group(q0, s):
        start = max(4 * q0 - 4, -2) + 2

        def pair(ref, comp, count):
            return jnp.concatenate(
                [jnp.broadcast_to(ref[comp, q0 + k, s:s + 1, :], (count, 128)) for k in range(2)], axis=1)

        col = pair(idx, 1, 1) + jnp.where(pair(idx, 0, 1) >= start + CUT, 64.0, 0.0)
        pick = jnp.where(iota_k == jnp.broadcast_to(col.astype(jnp.bfloat16), (128, 256)),
                         jnp.bfloat16(1.0), jnp.bfloat16(0.0))
        count = CUT + 2
        t = _dot(tables[s][24 * start:24 * (start + count), :], jnp.concatenate([pick, pick], axis=0))
        base = pair(idx, 0, 8) - (start * 1.0)
        base = jnp.where(base >= CUT, base - CUT, base)
        conds = []
        for cut in _levels(CUT):
            c = base >= cut
            conds.append((cut, c))
            base = jnp.where(c, base - cut, base)
        taps = []
        for b in range(3):
            T = [t[24 * k + 8 * b:24 * k + 8 * b + 8] for k in range(count)]
            for cut, c in conds:
                T = [jnp.where(c, T[k + cut], T[k]) if k + cut < len(T) else T[k] for k in range(cut + 2)]
            taps.append(T)
        fr, fc = pair(frac, 0, 8), pair(frac, 1, 8)
        A, B = [], []
        for a in range(3):
            w = fc * taps[2][a]
            v = taps[1][a] + w
            A.append(taps[0][a] + fc * v)
            B.append(v + w)
        da, qa = 0.5 * (A[2] - A[0]), 0.5 * (A[2] + A[0]) - A[1]
        db, qb = 0.5 * (B[2] - B[0]), 0.5 * (B[2] + B[0]) - B[1]
        wa = fr * qa
        va = da + wa
        warped = A[1] + 0.25 * qa + fr * va
        slope_row = va + wa
        slope_col = B[1] + 0.25 * qb + fr * (db + fr * qb)
        target = jnp.concatenate([targets[s][q0], targets[s][q0 + 1]], axis=1)
        miss = (warped - target) * (2.0 / CH)
        for comp, slope in ((0, slope_row), (1, slope_col)):
            total = jnp.sum(miss * slope, axis=0, keepdims=True)
            for k in range(2):
                dat[comp, q0 + k, s:s + 1, :] = total[:, 128 * k:128 * k + 128]

    def step(t):
        for q in range(NQ):
            y = 4 * q - 4 + lane // 32
            ok = col_in & (row0 + y >= 0) & (row0 + y < rows)
            for comp, origin in ((0, y + REACH + 2), (1, j + REACH)):
                v = jnp.tanh(raw[comp, q] * (1.0 / REACH))
                d = REACH * v
                n = jnp.floor(d + 0.5)
                sq[comp, q] = v
                disp[comp, q] = jnp.where(ok, d, 0.0)
                frac[comp, q] = d - n
                idx[comp, q] = n + origin.astype(jnp.float32)
        if t == 0:
            ready, spent = [(q0, s) for s in range(1, SEGS - 1) for q0 in range(0, NQ, 2)], 0
            for length in edges(ready):
                spent += length
                while spent >= PACE and ready:
                    spent -= PACE
                    group(*ready.pop(0))
            for at in ready:
                group(*at)
        for q0 in range(0, NQ, 2) if t < 2 else range(1, NQ - 1, 2):
            if t > 0:
                for s in range(SEGS):
                    group(q0, s)
            for comp in range(2):
                for q in (q0, q0 + 1):
                    update(t, comp, q)
                if t == 2:
                    finish(comp, q0 // 2)

    def update(t, comp, q):
        one, two = 1.0 / (1.0 - 0.9 ** (t + 1)), 1.0 / (1.0 - 0.999 ** (t + 1))
        d = disp[comp, q]
        up = jnp.where(lane < 96, _roll(d, -32, 1), _roll(disp[comp, min(q + 1, NQ - 1)], -32, 1))
        down = jnp.where(lane >= 32, _roll(d, 32, 1), _roll(disp[comp, max(q - 1, 0)], 32, 1))
        around = up + down + _roll(d, 1, 1) + _roll(d, -1, 1)
        v = sq[comp, q]
        grad = (dat[comp, q] + 2.0 * STIFFNESS * (4.0 * REACH * v - around)) * (1.0 - v * v)
        a, b = 0.1 * grad, 0.001 * grad * grad
        if t > 0:
            a, b = 0.9 * m1[comp, q] + a, 0.999 * m2[comp, q] + b
        m1[comp, q] = a
        m2[comp, q] = b
        raw[comp, q] = raw[comp, q] - STEP * (a * one) / (jnp.sqrt(b * two) + EPS)

    own = _own(own_ref)

    def finish(comp, b):
        out = None
        for s in range(SEGS):
            v = jnp.where(sub < 4, jnp.broadcast_to(raw[comp, 2 * b + 1, s:s + 1, :], (8, 128)),
                          jnp.broadcast_to(raw[comp, 2 * b + 2, s:s + 1, :], (8, 128)))
            v = _pick(v, (lane + 32 * (sub % 4) + (128 + SIDE - WIDE * s)) & 127)
            out = v if s == 0 else jnp.where(lane < WIDE * s, out, v)
        out_ref[comp, 8 * b:8 * b + 8] = out - own[2 + comp][8 * b:8 * b + 8]

    for t in range(ITERS):
        step(t)


def _swaps(n, first, wrap):
    return [p for a in range(first, n if wrap else n - 1, 2) for p in ((a, (a + 1) % n), ((a + 1) % n, a))]


def _exchange(pair, axis):
    n = lax.axis_size(axis)
    return [lax.ppermute(x, axis, _swaps(n, k, axis == "row")) for k, x in enumerate(pair)]


def _local(fixed_section, moving_section, field_init, first_weight, first_bias, second_weight):
    vmem = pl.BlockSpec(memory_space=pltpu.VMEM)
    smem = pl.BlockSpec(memory_space=pltpu.SMEM)
    anywhere = pl.BlockSpec(memory_space=pltpu.HBM)
    f32, bf16 = jnp.float32, jnp.bfloat16

    def call(body, name, out, specs, scratch):
        return pl.pallas_call(
            body,
            out_shape=[jax.ShapeDtypeStruct(*x) for x in out],
            in_specs=specs,
            out_specs=[vmem] * len(out),
            scratch_shapes=scratch,
            compiler_params=pltpu.CompilerParams(vmem_limit_bytes=48 * 2 ** 20),
            name=name,
        )

    strip = ((sum(PADS), 128), f32)
    one, two, own = call(_pack_rows, "pack_rows", [strip, strip, ((4 * TR, TC), f32)], [anywhere] * 3, [
        pltpu.VMEM((TR, TC), bf16), pltpu.VMEM((TR, TC), bf16), pltpu.VMEM((2, TR, TC), f32),
        pltpu.SemaphoreType.DMA((3,))])(*[pltpu.with_memory_space_constraint(x, pltpu.HBM) for x in (moving_section, fixed_section, field_init)])
    up, down = _exchange((one, two), "row")
    w1, w2, bias = call(_weights, "weights", [((128, 48), bf16), ((384, 160), bf16), ((CH, 128), f32)],
                        [anywhere, anywhere, smem], [
        pltpu.VMEM((CH, 9), f32), pltpu.VMEM((CH, CH, 9), f32), pltpu.VMEM((2, CH, 128), f32),
        pltpu.SemaphoreType.DMA((2,))])(*[pltpu.with_memory_space_constraint(x, pltpu.HBM) for x in (first_weight, second_weight)], first_bias)
    strip = ((8 * pl.cdiv(TALL, 32), 128), f32)
    one, two = _exchange(call(_pack_cols, "pack_cols", [strip, strip], [vmem] * 4, [])(own, up, down, bias), "col")
    hidden = pltpu.VMEM((2, HROWS * CH, 256), bf16)
    table, target = (PROWS * 24, 256), (NQ, CH, 128)
    mid = call(_middle, "middle", [
        ((SEGS - 2,) + table, bf16), ((SEGS - 2,) + target, f32), ((2, NQ, 8, 128), f32), ((2, EROWS, CH, 128), f32),
    ], [vmem] * 6, [hidden])(own, up, down, w1, bias, w2)
    return call(_refine, "refine", [((2, TR, TC), f32)], [vmem] * 12, [
        hidden, pltpu.VMEM((2,) + table, bf16), pltpu.VMEM((2,) + target, f32),
        *[pltpu.VMEM((2, NQ, 8, 128), f32) for _ in range(8)],
    ])(own, up, down, one, two, w1, bias, w2, *mid)[0]


def solution(mesh):
    return jax.shard_map(
        _local,
        mesh=mesh,
        in_specs=(P("row", "col"), P("row", "col"), P(None, "row", "col"), P(), P(), P()),
        out_specs=P(None, "row", "col"),
        check_vma=False,
    )
```

```python
import jax
import jax.numpy as jnp
from jax import lax
from jax.experimental import pallas as pl
from jax.experimental.pallas import tpu as pltpu
from jax.sharding import PartitionSpec as P

CH = 8
REACH = 16
ITERS = 3
STIFFNESS = 0.01
STEP = 0.5
EPS = 0.01

TR, TC = 32, 128
SIDE = 3
HALO_M = REACH + 1 + 2 + 2
HALO_PAD = 24
PADS = (HALO_PAD, 8, 8, 8)
TALL = TR + 2 * HALO_PAD
WIDTHS = (HALO_M, 4, SIDE, SIDE)
STRIPS = (0, HALO_M, HALO_M + 4, HALO_M + 4 + SIDE)
EROWS = 72
HROWS = 80
TOP = -(REACH + 3)
BLOCKS = EROWS // 8
FIXED_BLOCKS = range(2, 7)

SEGS = 5
WIDE = 26
NQ = 10
CUT = 20
PROWS = EROWS - CUT


FROM0 = REACH + 3
FAR = 117
PACE = 300
HALF = 5
AT4 = 62
FROM4 = WIDE * (SEGS - 1) - FROM0 - AT4


def _levels(span):
    out = []
    while span > 1:
        cut = (span + 1) // 2
        out.append(cut)
        span = cut
    return out


def _split(x):
    hi = x.astype(jnp.bfloat16)
    lo = (x - hi.astype(jnp.float32)).astype(jnp.bfloat16)
    return hi, lo


def _roll(x, shift, axis):
    size = x.shape[axis]
    shift = shift % size
    return x if shift == 0 else pltpu.roll(x, shift, axis)


def _pick(x, index):
    dims = lax.GatherDimensionNumbers(
        offset_dims=(), collapsed_slice_dims=(1,), start_index_map=(1,),
        operand_batching_dims=(0,), start_indices_batching_dims=(0,))
    return lax.gather(x, index[..., None], dims, (1, 1), mode=lax.GatherScatterMode.PROMISE_IN_BOUNDS)


def _dot(a, b):
    return jnp.dot(a, b, preferred_element_type=jnp.float32)


def _tall(own, one, two):
    r, n = lax.axis_index("row"), lax.axis_size("row")
    even = lax.rem(r, 2) == 0
    above = jnp.where(r > 0, jnp.where(even, two, one), 0.0)
    below = jnp.where(r < n - 1, jnp.where(even, one, two), 0.0)
    out, at = [], 0
    for x, pad in zip(own, PADS):
        out.append(jnp.concatenate([above[at:at + pad], x, below[at:at + pad]], axis=0))
        at += pad
    return out


def _fetch(pairs, sems):
    copies = [pltpu.make_async_copy(src, dst, sems.at[k]) for k, (src, dst) in enumerate(pairs)]
    for copy in copies:
        copy.start()
    for copy in copies:
        copy.wait()


def _own(own_ref):
    return [own_ref[TR * k:TR * k + TR] for k in range(4)]


def _pack_rows(mv_ref, fx_ref, fd_ref, one_ref, two_ref, own_ref, mv, fx, fd, sems):
    _fetch([(mv_ref, mv), (fx_ref, fx), (fd_ref, fd)], sems)
    even = lax.rem(lax.axis_index("row"), 2) == 0
    at = 0
    for k, x in enumerate([mv[...].astype(jnp.float32), fx[...].astype(jnp.float32), fd[0], fd[1]]):
        pad = PADS[k]
        own_ref[TR * k:TR * k + TR] = x
        first, last = x[:pad], x[TR - pad:]
        one_ref[at:at + pad] = jnp.where(even, last, first)
        two_ref[at:at + pad] = jnp.where(even, first, last)
        at += pad


def _weights(w1_ref, w2_ref, bias_ref, m1_ref, m2_ref, b_ref, w1, w2, flat, sems):
    _fetch([(w1_ref, w1), (w2_ref, w2)], sems)
    lane = lax.broadcasted_iota(jnp.int32, (CH, 128), 1)
    sub = lax.broadcasted_iota(jnp.int32, (CH, 128), 0)
    flat[0] = jnp.zeros((CH, 128), jnp.float32)
    flat[1] = jnp.zeros((CH, 128), jnp.float32)
    flat[0, :, 0:9] = w1[...]
    for c2 in range(CH):
        flat[1, :, 9 * c2:9 * c2 + 9] = w2[:, c2, :]
    b = jnp.zeros((CH, 128), jnp.float32)
    for c in range(CH):
        b = jnp.where(sub == c, bias_ref[c], b)
    b_ref[...] = b
    hi_rows, lo_rows = [], []
    for y in range(8):
        ky = lane % 16 - y - (HALO_PAD - HALO_M)
        v = _pick(flat[0], jnp.clip(3 * ky + lane // 16, 0, 127))
        v = jnp.where((ky >= 0) & (ky <= 2), v, 0.0)
        hi = v.astype(jnp.bfloat16).astype(jnp.float32)
        hi_rows.append(hi)
        lo_rows.append(v - hi)
    m1_ref[...] = jnp.concatenate(hi_rows + lo_rows, axis=0)[:, :48].astype(jnp.bfloat16)
    hi_rows, lo_rows = [], []
    for kx in range(3):
        for y in range(8):
            halves = []
            for half in range(2):
                at = lane + 128 * half
                at = jnp.where(at >= 80, at - 80, at)
                ky = at // 8 - y
                v = _pick(flat[1], jnp.clip(9 * (at % 8) + 3 * ky + kx, 0, 127))
                halves.append(jnp.where((ky >= 0) & (ky <= 2), v, 0.0))
            v = jnp.concatenate(halves, axis=1)
            hi = v.astype(jnp.bfloat16).astype(jnp.float32)
            wide = lax.broadcasted_iota(jnp.int32, (CH, 256), 1)
            hi_rows.append(hi)
            lo_rows.append(jnp.where(wide < 80, v - hi, 0.0))
    m2_ref[...] = jnp.concatenate(hi_rows + lo_rows, axis=0)[:, :160].astype(jnp.bfloat16)


def _pack_cols(own_ref, down_ref, up_ref, _, one_ref, two_ref):
    even = lax.rem(lax.axis_index("col"), 2) == 0
    tall = _tall(_own(own_ref), up_ref[...], down_ref[...])
    lane = lax.broadcasted_iota(jnp.int32, (8, 128), 1)
    for i in range(0, TALL // 8, 4):
        first = last = jnp.zeros((8, 128), jnp.float32)
        for b in range(i, min(i + 4, TALL // 8)):
            for k, x in enumerate(tall):
                if 8 * b < x.shape[0]:
                    v, at = x[8 * b:8 * b + 8], 32 * (b - i) + STRIPS[k]
                    first = jnp.where(lane < at, first, _roll(v, at, 1))
                    last = jnp.where(lane < at, last, _roll(v, at + WIDTHS[k], 1))
        one_ref[2 * i:2 * i + 8] = jnp.where(even, last, first)
        two_ref[2 * i:2 * i + 8] = jnp.where(even, first, last)


def _unpack(x):
    return jnp.concatenate([_roll(x[8 * (b // 4):8 * (b // 4) + 8], -32 * (b % 4), 1) for b in range(TALL // 8)], axis=0)


def _edges(own, up, down, one, two):
    c, n = lax.axis_index("col"), lax.axis_size("col")
    even = lax.rem(c, 2) == 0
    left = _unpack(jnp.where(c > 0, jnp.where(even, two, one), 0.0))
    right = _unpack(jnp.where(c < n - 1, jnp.where(even, one, two), 0.0))
    tall = _tall(own, up, down)
    images = []
    for k, x in enumerate(tall[:2]):
        lane = lax.broadcasted_iota(jnp.int32, x.shape, 1) - 64 * k
        r = x.shape[0]
        v = jnp.where(lane < 32 + TC - FAR, _roll(x, 64 * k + 32 - FAR, 1), _roll(right[:r], 64 * k + 32 + TC - FAR - STRIPS[k], 1))
        v = jnp.where(lane < 32, _roll(x, 64 * k + HALO_M, 1), v)
        images.append(jnp.where(lane < HALO_M, _roll(left[:r], 64 * k + HALO_M - WIDTHS[k] - STRIPS[k], 1), v))
    blank = jnp.zeros((16, 128), jnp.float32)
    fixed = jnp.concatenate([blank, images[1], blank], axis=0)
    lane = lax.broadcasted_iota(jnp.int32, fixed.shape, 1)
    out = [jnp.where(lane < 64, images[0], fixed)]
    for k in (2, 3):
        x = tall[k]
        lane = lax.broadcasted_iota(jnp.int32, x.shape, 1)
        r = x.shape[0]
        v = jnp.where(lane < TC - FROM4, _roll(x, -FROM4, 1), _roll(right[:r], TC - FROM4 - STRIPS[k], 1))
        v = jnp.where(lane < AT4, _roll(x, FROM0, 1), v)
        out.append(jnp.where(lane < FROM0, _roll(left[:r], FROM0 - WIDTHS[k] - STRIPS[k], 1), v))
    return out


class _Place:
    def __init__(self):
        self.row, self.col = TR * lax.axis_index("row"), TC * lax.axis_index("col")
        self.rows, self.cols = TR * lax.axis_size("row"), TC * lax.axis_size("col")

    def keep(self, y, col_ok):
        r = self.row + y
        ok = jnp.where((r >= 0) & (r < self.rows), 1, 0)
        return jnp.where(col_ok, ok.astype(jnp.float32), 0.0)


def _embed(place, images, column, tops, blocks, w1_ref, bias_ref, w2_ref, hs, sink):
    bias = bias_ref[...]
    x = place.col + column
    col_ok = (x >= 0) & (x < place.cols)
    shifted = [jnp.concatenate([_roll(v, 1 - kx, 1) for v in images], axis=1) for kx in range(3)]
    count = max(max(b) for b in blocks) + 1
    for b in range(count + 1):
        if 8 * b + 16 > shifted[0].shape[0]:
            hs[:, 64 * b:64 * b + 64, :] = jnp.zeros((2, 64, 256), jnp.bfloat16)
            continue
        t = _dot(w1_ref[...], jnp.concatenate([v[8 * b:8 * b + 16] for v in shifted], axis=0).astype(jnp.bfloat16))
        pre = t[:64] + t[64:]
        for h in range(2):
            at = slice(128 * h, 128 * h + 128)
            if b not in blocks[h] and b - 1 not in blocks[h]:
                hs[:, 64 * b:64 * b + 64, at] = jnp.zeros((2, 64, 128), jnp.bfloat16)
                continue
            v = jnp.concatenate([
                jnp.maximum(pre[CH * k:CH * k + CH, at] + bias, 0.0) * place.keep(tops[h] - 1 + 8 * b + k, col_ok)
                for k in range(8)], axis=0)
            hs[0, 64 * b:64 * b + 64, at], hs[1, 64 * b:64 * b + 64, at] = _split(v)
        yield 100
    for b in range(count):
        t = _dot(w2_ref[...], jnp.concatenate([hs[0, 64 * b:64 * b + 80], hs[1, 64 * b:64 * b + 80]], axis=0))
        v = t[:192] + t[192:]
        for h in range(2):
            if b not in blocks[h]:
                continue
            o = [v[64 * kx:64 * kx + 64, 128 * h:128 * h + 128] for kx in range(3)]
            e = o[1] + _roll(o[0], 1, 1) + _roll(o[2], -1, 1)
            sink(b, h, [e[CH * k:CH * k + CH] * place.keep(tops[h] + 8 * b + k, col_ok) for k in range(8)])
        yield 120


def _build(moving, fixed, window, pixel, e3, ef):
    lane = lax.broadcasted_iota(jnp.int32, (8, 128), 1)
    for r in range(0, PROWS, 2):
        out = []
        for k in (r, r + 1):
            e0 = jnp.where(lane < 64, _roll(moving[k], -window, 1), _roll(moving[k + CUT], 64 - window, 1))
            left, right = _roll(e0, 1, 1), _roll(e0, -1, 1)
            p1 = 0.5 * (right - left)
            p2 = 0.5 * (right + left) - e0
            out += [e0 + 0.25 * p2, p1, p2]
        hi, lo = _split(jnp.concatenate(out, axis=0))
        e3[24 * r:24 * r + 48, 0:128] = hi
        e3[24 * r:24 * r + 48, 128:256] = lo
        yield 25
    for q in range(NQ):
        cur = None
        for i in range(4):
            row = min(max(4 * q - 4 + i, -2), TR + 1) - TOP
            v = _roll(fixed[row], 32 * i - pixel, 1)
            cur = v if i == 0 else jnp.where(lane < 32 * i, cur, v)
        ef[q] = cur
        yield 25


def _start(field, pixel, s, raw):
    lane = lax.broadcasted_iota(jnp.int32, (8, 128), 1)
    sub = lax.broadcasted_iota(jnp.int32, (8, 128), 0)
    mine = lane // 32 == sub % 4
    for comp in range(2):
        for b in range(NQ // 2):
            v = field[comp][8 * b + 4:8 * b + 12]
            v = _pick(v, (lane - 32 * (sub % 4) + pixel) & 127)
            for k in range(2):
                raw[comp, 2 * b + k, s:s + 1, :] = jnp.sum(
                    jnp.where(mine & (sub // 4 == k), v, 0.0), axis=0, keepdims=True)


def _middle(own_ref, down_ref, up_ref, w1_ref, bias_ref, w2_ref, e3_ref, ef_ref, raw_ref, rows_ref, hs):
    moving, fixed, *field = _tall(_own(own_ref), up_ref[...], down_ref[...])
    lane = lax.broadcasted_iota(jnp.int32, (CH, 128), 1)
    rows = [{}, {}]

    def sink(b, h, got):
        for k, v in enumerate(got):
            rows[h][8 * b + k] = v
            rows_ref[h, 8 * b + k] = v

    blank = jnp.zeros((16, 128), jnp.float32)
    fixed = jnp.concatenate([blank, fixed, blank], axis=0)
    for _ in _embed(_Place(), [moving, fixed], lane, [TOP, TOP], [range(BLOCKS), FIXED_BLOCKS],
                    w1_ref, bias_ref, w2_ref, hs, sink):
        pass
    raw_ref[...] = jnp.zeros_like(raw_ref)
    for s in range(1, SEGS - 1):
        _start(field, WIDE * s - SIDE, s, raw_ref)
        for _ in _build(rows[0], rows[1], WIDE * s - 3 - REACH, WIDE * s - SIDE, e3_ref.at[s - 1], ef_ref.at[s - 1]):
            pass


def _refine(own_ref, down_ref, up_ref, one_ref, two_ref, w1_ref, bias_ref, w2_ref, mid3_ref, midf_ref, midr_ref, rows_ref,
            out_ref, hs, e3, ef, raw, m1, m2, sq, disp, frac, idx, dat):
    place = _Place()
    row0, col0, rows, cols = place.row, place.col, place.rows, place.cols
    lane = lax.broadcasted_iota(jnp.int32, (8, 128), 1)
    sub = lax.broadcasted_iota(jnp.int32, (8, 128), 0)
    image, *field = _edges(_own(own_ref), up_ref[...], down_ref[...], one_ref[...], two_ref[...])
    raw[...] = midr_ref[...]
    _start(field, REACH, 0, raw)
    _start(field, AT4 + REACH, SEGS - 1, raw)
    tables = [e3.at[0]] + [mid3_ref.at[k] for k in range(SEGS - 2)] + [e3.at[1]]
    targets = [ef.at[0]] + [midf_ref.at[k] for k in range(SEGS - 2)] + [ef.at[1]]

    def edges(ready):
        rows = [[{}, {}], [{}, {}]]

        def sink(b, h, got):
            for k, v in enumerate(got):
                r = 8 * (b + HALF * h) + k
                mine = rows_ref[0, r]
                rows[0][0][r] = jnp.where(lane < FROM0 + 2, _roll(v, FROM0 - HALO_M, 1), _roll(mine, FROM0, 1))
                rows[1][0][r] = jnp.where(lane < TC - FROM4 - 2, _roll(mine, -FROM4, 1), _roll(v, FAR - 32 - FROM4, 1))
                if r // 8 in FIXED_BLOCKS:
                    mine = rows_ref[1, r]
                    rows[0][1][r] = jnp.where(lane < FROM0 + 2, _roll(v, FROM0 - HALO_M - 64, 1), _roll(mine, FROM0, 1))
                    rows[1][1][r] = jnp.where(lane < TC - FROM4 - 2, _roll(mine, -FROM4, 1), _roll(v, FAR - 96 - FROM4, 1))

        column = jnp.where(lane % 64 < 32, lane % 32 - HALO_M, lane % 32 + FAR)
        blank = jnp.zeros((8, 128), jnp.float32)
        halves = [image[:8 * HALF + 16], jnp.concatenate([image[8 * HALF:], blank, blank], axis=0)]
        yield from _embed(place, halves, column, [TOP, TOP + 8 * HALF], [range(HALF), range(BLOCKS - HALF)],
                          w1_ref, bias_ref, w2_ref, hs, sink)
        yield from _build(rows[0][0], rows[0][1], 0, REACH, e3.at[0], ef.at[0])
        ready.extend((q0, 0) for q0 in range(0, NQ, 2))
        yield from _build(rows[1][0], rows[1][1], AT4, AT4 + REACH, e3.at[1], ef.at[1])
        ready.extend((q0, SEGS - 1) for q0 in range(0, NQ, 2))

    dat[...] = jnp.zeros_like(dat)

    j = lane % 32
    x = col0 + WIDE * sub - SIDE + j
    col_in = (x >= 0) & (x < cols)
    iota_k = lax.broadcasted_iota(jnp.int32, (128, 256), 0).astype(jnp.float32).astype(jnp.bfloat16)

    def group(q0, s):
        start = max(4 * q0 - 4, -2) + 2

        def pair(ref, comp, count):
            return jnp.concatenate(
                [jnp.broadcast_to(ref[comp, q0 + k, s:s + 1, :], (count, 128)) for k in range(2)], axis=1)

        col = pair(idx, 1, 1) + jnp.where(pair(idx, 0, 1) >= start + CUT, 64.0, 0.0)
        pick = jnp.where(iota_k == jnp.broadcast_to(col.astype(jnp.bfloat16), (128, 256)),
                         jnp.bfloat16(1.0), jnp.bfloat16(0.0))
        count = CUT + 2
        t = _dot(tables[s][24 * start:24 * (start + count), :], jnp.concatenate([pick, pick], axis=0))
        base = pair(idx, 0, 8) - (start * 1.0)
        base = jnp.where(base >= CUT, base - CUT, base)
        conds = []
        for cut in _levels(CUT):
            c = base >= cut
            conds.append((cut, c))
            base = jnp.where(c, base - cut, base)
        taps = []
        for b in range(3):
            T = [t[24 * k + 8 * b:24 * k + 8 * b + 8] for k in range(count)]
            for cut, c in conds:
                T = [jnp.where(c, T[k + cut], T[k]) if k + cut < len(T) else T[k] for k in range(cut + 2)]
            taps.append(T)
        fr, fc = pair(frac, 0, 8), pair(frac, 1, 8)
        A, B = [], []
        for a in range(3):
            w = fc * taps[2][a]
            v = taps[1][a] + w
            A.append(taps[0][a] + fc * v)
            B.append(v + w)
        da, qa = 0.5 * (A[2] - A[0]), 0.5 * (A[2] + A[0]) - A[1]
        db, qb = 0.5 * (B[2] - B[0]), 0.5 * (B[2] + B[0]) - B[1]
        wa = fr * qa
        va = da + wa
        warped = A[1] + 0.25 * qa + fr * va
        slope_row = va + wa
        slope_col = B[1] + 0.25 * qb + fr * (db + fr * qb)
        target = jnp.concatenate([targets[s][q0], targets[s][q0 + 1]], axis=1)
        miss = (warped - target) * (2.0 / CH)
        for comp, slope in ((0, slope_row), (1, slope_col)):
            total = jnp.sum(miss * slope, axis=0, keepdims=True)
            for k in range(2):
                dat[comp, q0 + k, s:s + 1, :] = total[:, 128 * k:128 * k + 128]

    def step(t):
        for q in range(NQ):
            y = 4 * q - 4 + lane // 32
            ok = col_in & (row0 + y >= 0) & (row0 + y < rows)
            for comp, origin in ((0, y + REACH + 2), (1, j + REACH)):
                v = jnp.tanh(raw[comp, q] * (1.0 / REACH))
                d = REACH * v
                n = jnp.floor(d + 0.5)
                sq[comp, q] = v
                disp[comp, q] = jnp.where(ok, d, 0.0)
                frac[comp, q] = d - n
                idx[comp, q] = n + origin.astype(jnp.float32)
        if t == 0:
            ready, spent = [(q0, s) for s in range(1, SEGS - 1) for q0 in range(0, NQ, 2)], 0
            for length in edges(ready):
                spent += length
                while spent >= PACE and ready:
                    spent -= PACE
                    group(*ready.pop(0))
            for at in ready:
                group(*at)
        for q0 in range(0, NQ, 2) if t < 2 else range(1, NQ - 1, 2):
            if t > 0:
                for s in range(SEGS):
                    group(q0, s)
            for comp in range(2):
                for q in (q0, q0 + 1):
                    update(t, comp, q)
                if t == 2:
                    finish(comp, q0 // 2)

    def update(t, comp, q):
        one, two = 1.0 / (1.0 - 0.9 ** (t + 1)), 1.0 / (1.0 - 0.999 ** (t + 1))
        d = disp[comp, q]
        up = jnp.where(lane < 96, _roll(d, -32, 1), _roll(disp[comp, min(q + 1, NQ - 1)], -32, 1))
        down = jnp.where(lane >= 32, _roll(d, 32, 1), _roll(disp[comp, max(q - 1, 0)], 32, 1))
        around = up + down + _roll(d, 1, 1) + _roll(d, -1, 1)
        v = sq[comp, q]
        grad = (dat[comp, q] + 2.0 * STIFFNESS * (4.0 * REACH * v - around)) * (1.0 - v * v)
        a, b = 0.1 * grad, 0.001 * grad * grad
        if t > 0:
            a, b = 0.9 * m1[comp, q] + a, 0.999 * m2[comp, q] + b
        m1[comp, q] = a
        m2[comp, q] = b
        raw[comp, q] = raw[comp, q] - STEP * (a * one) / (jnp.sqrt(b * two) + EPS)

    own = _own(own_ref)

    def finish(comp, b):
        out = None
        for s in range(SEGS):
            v = jnp.where(sub < 4, jnp.broadcast_to(raw[comp, 2 * b + 1, s:s + 1, :], (8, 128)),
                          jnp.broadcast_to(raw[comp, 2 * b + 2, s:s + 1, :], (8, 128)))
            v = _pick(v, (lane + 32 * (sub % 4) + (128 + SIDE - WIDE * s)) & 127)
            out = v if s == 0 else jnp.where(lane < WIDE * s, out, v)
        out_ref[comp, 8 * b:8 * b + 8] = out - own[2 + comp][8 * b:8 * b + 8]

    for t in range(ITERS):
        step(t)


def _swaps(axis, first):
    rows, cols = lax.axis_size("row"), lax.axis_size("col")
    n = rows if axis == "row" else cols
    out = []
    for r in range(rows):
        for c in range(cols):
            i = r if axis == "row" else c
            j = i + 1 if (i - first) % 2 == 0 else i - 1
            if 0 <= j < n:
                r2, c2 = (j, c) if axis == "row" else (r, j)
            elif axis == "row":
                r2, c2 = r, c ^ 1
            else:
                r2, c2 = r ^ 1, c
            out.append((r * cols + c, r2 * cols + c2))
    return out


def _exchange(pair, axis):
    return [lax.ppermute(x, ("row", "col"), _swaps(axis, k)) for k, x in enumerate(pair)]


def _local(fixed_section, moving_section, field_init, first_weight, first_bias, second_weight):
    vmem = pl.BlockSpec(memory_space=pltpu.VMEM)
    smem = pl.BlockSpec(memory_space=pltpu.SMEM)
    anywhere = pl.BlockSpec(memory_space=pltpu.HBM)
    f32, bf16 = jnp.float32, jnp.bfloat16

    def call(body, name, out, specs, scratch):
        return pl.pallas_call(
            body,
            out_shape=[jax.ShapeDtypeStruct(*x) for x in out],
            in_specs=specs,
            out_specs=[vmem] * len(out),
            scratch_shapes=scratch,
            compiler_params=pltpu.CompilerParams(vmem_limit_bytes=48 * 2 ** 20),
            name=name,
        )

    strip = ((sum(PADS), 128), f32)
    one, two, own = call(_pack_rows, "pack_rows", [strip, strip, ((4 * TR, TC), f32)], [anywhere] * 3, [
        pltpu.VMEM((TR, TC), bf16), pltpu.VMEM((TR, TC), bf16), pltpu.VMEM((2, TR, TC), f32),
        pltpu.SemaphoreType.DMA((3,))])(*[pltpu.with_memory_space_constraint(x, pltpu.HBM) for x in (moving_section, fixed_section, field_init)])
    up, down = _exchange((one, two), "row")
    w1, w2, bias = call(_weights, "weights", [((128, 48), bf16), ((384, 160), bf16), ((CH, 128), f32)],
                        [anywhere, anywhere, smem], [
        pltpu.VMEM((CH, 9), f32), pltpu.VMEM((CH, CH, 9), f32), pltpu.VMEM((2, CH, 128), f32),
        pltpu.SemaphoreType.DMA((2,))])(*[pltpu.with_memory_space_constraint(x, pltpu.HBM) for x in (first_weight, second_weight)], first_bias)
    strip = ((8 * pl.cdiv(TALL, 32), 128), f32)
    one, two = _exchange(call(_pack_cols, "pack_cols", [strip, strip], [vmem] * 4, [])(own, down, up, bias), "col")
    hidden = pltpu.VMEM((2, HROWS * CH, 256), bf16)
    table, target = (PROWS * 24, 256), (NQ, CH, 128)
    mid = call(_middle, "middle", [
        ((SEGS - 2,) + table, bf16), ((SEGS - 2,) + target, f32), ((2, NQ, 8, 128), f32), ((2, EROWS, CH, 128), f32),
    ], [vmem] * 6, [hidden])(own, down, up, w1, bias, w2)
    return call(_refine, "refine", [((2, TR, TC), f32)], [vmem] * 12, [
        hidden, pltpu.VMEM((2,) + table, bf16), pltpu.VMEM((2,) + target, f32),
        *[pltpu.VMEM((2, NQ, 8, 128), f32) for _ in range(8)],
    ])(own, down, up, one, two, w1, bias, w2, *mid)[0]


def solution(mesh):
    return jax.shard_map(
        _local,
        mesh=mesh,
        in_specs=(P("row", "col"), P("row", "col"), P(None, "row", "col"), P(), P(), P()),
        out_specs=P(None, "row", "col"),
        check_vma=False,
    )
```

```python
import jax
import jax.numpy as jnp
from jax import lax
from jax.experimental import pallas as pl
from jax.experimental.pallas import tpu as pltpu
from jax.sharding import PartitionSpec as P

CH = 8
REACH = 16
ITERS = 3
STIFFNESS = 0.01
STEP = 0.5
EPS = 0.01

TR, TC = 32, 128
SIDE = 3
HALO_M = REACH + 1 + 2 + 2
HALO_PAD = 24
PADS = (HALO_PAD, 8, 8, 8)
TALL = TR + 2 * HALO_PAD
WIDTHS = (HALO_M, 4, SIDE, SIDE)
STRIPS = (0, HALO_M, HALO_M + 4, HALO_M + 4 + SIDE)
EROWS = 72
HROWS = 80
TOP = -(REACH + 3)
BLOCKS = EROWS // 8
FIXED_BLOCKS = range(2, 7)

SEGS = 5
WIDE = 26
NQ = 10
CUT = 20
PROWS = EROWS - CUT


FROM0 = REACH + 3
FAR = 117
PACE = 300
HALF = 5
AT4 = 62
FROM4 = WIDE * (SEGS - 1) - FROM0 - AT4


def _levels(span):
    out = []
    while span > 1:
        cut = (span + 1) // 2
        out.append(cut)
        span = cut
    return out


def _split(x):
    hi = x.astype(jnp.bfloat16)
    lo = (x - hi.astype(jnp.float32)).astype(jnp.bfloat16)
    return hi, lo


def _roll(x, shift, axis):
    size = x.shape[axis]
    shift = shift % size
    return x if shift == 0 else pltpu.roll(x, shift, axis)


def _pick(x, index):
    dims = lax.GatherDimensionNumbers(
        offset_dims=(), collapsed_slice_dims=(1,), start_index_map=(1,),
        operand_batching_dims=(0,), start_indices_batching_dims=(0,))
    return lax.gather(x, index[..., None], dims, (1, 1), mode=lax.GatherScatterMode.PROMISE_IN_BOUNDS)


def _dot(a, b):
    return jnp.dot(a, b, preferred_element_type=jnp.float32)


def _tall(own, one, two):
    r, n = lax.axis_index("row"), lax.axis_size("row")
    even = lax.rem(r, 2) == 0
    above = jnp.where(r > 0, jnp.where(even, two, one), 0.0)
    below = jnp.where(r < n - 1, jnp.where(even, one, two), 0.0)
    out, at = [], 0
    for x, pad in zip(own, PADS):
        out.append(jnp.concatenate([above[at:at + pad], x, below[at:at + pad]], axis=0))
        at += pad
    return out


def _fetch(pairs, sems):
    copies = [pltpu.make_async_copy(src, dst, sems.at[k]) for k, (src, dst) in enumerate(pairs)]
    for copy in copies:
        copy.start()
    for copy in copies:
        copy.wait()


def _own(own_ref):
    return [own_ref[TR * k:TR * k + TR] for k in range(4)]


def _pack_rows(mv_ref, fx_ref, fd_ref, one_ref, two_ref, own_ref, mv, fx, fd, sems):
    _fetch([(mv_ref, mv), (fx_ref, fx), (fd_ref, fd)], sems)
    even = lax.rem(lax.axis_index("row"), 2) == 0
    at = 0
    for k, x in enumerate([mv[...].astype(jnp.float32), fx[...].astype(jnp.float32), fd[0], fd[1]]):
        pad = PADS[k]
        own_ref[TR * k:TR * k + TR] = x
        first, last = x[:pad], x[TR - pad:]
        one_ref[at:at + pad] = jnp.where(even, last, first)
        two_ref[at:at + pad] = jnp.where(even, first, last)
        at += pad


def _weights(w1_ref, w2_ref, bias_ref, m1_ref, m2_ref, b_ref, w1, w2, flat, sems):
    _fetch([(w1_ref, w1), (w2_ref, w2)], sems)
    lane = lax.broadcasted_iota(jnp.int32, (CH, 128), 1)
    sub = lax.broadcasted_iota(jnp.int32, (CH, 128), 0)
    flat[0] = jnp.zeros((CH, 128), jnp.float32)
    flat[1] = jnp.zeros((CH, 128), jnp.float32)
    flat[0, :, 0:9] = w1[...]
    for c2 in range(CH):
        flat[1, :, 9 * c2:9 * c2 + 9] = w2[:, c2, :]
    b = jnp.zeros((CH, 128), jnp.float32)
    for c in range(CH):
        b = jnp.where(sub == c, bias_ref[c], b)
    b_ref[...] = b
    hi_rows, lo_rows = [], []
    for y in range(8):
        ky = lane % 16 - y - (HALO_PAD - HALO_M)
        v = _pick(flat[0], jnp.clip(3 * ky + lane // 16, 0, 127))
        v = jnp.where((ky >= 0) & (ky <= 2), v, 0.0)
        hi = v.astype(jnp.bfloat16).astype(jnp.float32)
        hi_rows.append(hi)
        lo_rows.append(v - hi)
    m1_ref[...] = jnp.concatenate(hi_rows + lo_rows, axis=0)[:, :48].astype(jnp.bfloat16)
    hi_rows, lo_rows = [], []
    for kx in range(3):
        for y in range(8):
            halves = []
            for half in range(2):
                at = lane + 128 * half
                at = jnp.where(at >= 80, at - 80, at)
                ky = at // 8 - y
                v = _pick(flat[1], jnp.clip(9 * (at % 8) + 3 * ky + kx, 0, 127))
                halves.append(jnp.where((ky >= 0) & (ky <= 2), v, 0.0))
            v = jnp.concatenate(halves, axis=1)
            hi = v.astype(jnp.bfloat16).astype(jnp.float32)
            wide = lax.broadcasted_iota(jnp.int32, (CH, 256), 1)
            hi_rows.append(hi)
            lo_rows.append(jnp.where(wide < 80, v - hi, 0.0))
    m2_ref[...] = jnp.concatenate(hi_rows + lo_rows, axis=0)[:, :160].astype(jnp.bfloat16)


def _pack_cols(own_ref, up_ref, down_ref, _, one_ref, two_ref):
    even = lax.rem(lax.axis_index("col"), 2) == 0
    tall = _tall(_own(own_ref), up_ref[...], down_ref[...])
    lane = lax.broadcasted_iota(jnp.int32, (8, 128), 1)
    for i in range(0, TALL // 8, 4):
        first = last = jnp.zeros((8, 128), jnp.float32)
        for b in range(i, min(i + 4, TALL // 8)):
            for k, x in enumerate(tall):
                if 8 * b < x.shape[0]:
                    v, at = x[8 * b:8 * b + 8], 32 * (b - i) + STRIPS[k]
                    first = jnp.where(lane < at, first, _roll(v, at, 1))
                    last = jnp.where(lane < at, last, _roll(v, at + WIDTHS[k], 1))
        one_ref[2 * i:2 * i + 8] = jnp.where(even, last, first)
        two_ref[2 * i:2 * i + 8] = jnp.where(even, first, last)


def _unpack(x):
    return jnp.concatenate([_roll(x[8 * (b // 4):8 * (b // 4) + 8], -32 * (b % 4), 1) for b in range(TALL // 8)], axis=0)


def _edges(own, up, down, one, two):
    c, n = lax.axis_index("col"), lax.axis_size("col")
    even = lax.rem(c, 2) == 0
    left = _unpack(jnp.where(c > 0, jnp.where(even, two, one), 0.0))
    right = _unpack(jnp.where(c < n - 1, jnp.where(even, one, two), 0.0))
    tall = _tall(own, up, down)
    images = []
    for k, x in enumerate(tall[:2]):
        lane = lax.broadcasted_iota(jnp.int32, x.shape, 1) - 64 * k
        r = x.shape[0]
        v = jnp.where(lane < 32 + TC - FAR, _roll(x, 64 * k + 32 - FAR, 1), _roll(right[:r], 64 * k + 32 + TC - FAR - STRIPS[k], 1))
        v = jnp.where(lane < 32, _roll(x, 64 * k + HALO_M, 1), v)
        images.append(jnp.where(lane < HALO_M, _roll(left[:r], 64 * k + HALO_M - WIDTHS[k] - STRIPS[k], 1), v))
    blank = jnp.zeros((16, 128), jnp.float32)
    fixed = jnp.concatenate([blank, images[1], blank], axis=0)
    lane = lax.broadcasted_iota(jnp.int32, fixed.shape, 1)
    out = [jnp.where(lane < 64, images[0], fixed)]
    for k in (2, 3):
        x = tall[k]
        lane = lax.broadcasted_iota(jnp.int32, x.shape, 1)
        r = x.shape[0]
        v = jnp.where(lane < TC - FROM4, _roll(x, -FROM4, 1), _roll(right[:r], TC - FROM4 - STRIPS[k], 1))
        v = jnp.where(lane < AT4, _roll(x, FROM0, 1), v)
        out.append(jnp.where(lane < FROM0, _roll(left[:r], FROM0 - WIDTHS[k] - STRIPS[k], 1), v))
    return out


class _Place:
    def __init__(self):
        self.row, self.col = TR * lax.axis_index("row"), TC * lax.axis_index("col")
        self.rows, self.cols = TR * lax.axis_size("row"), TC * lax.axis_size("col")

    def keep(self, y, col_ok):
        r = self.row + y
        ok = jnp.where((r >= 0) & (r < self.rows), 1, 0)
        return jnp.where(col_ok, ok.astype(jnp.float32), 0.0)


def _embed(place, images, column, tops, blocks, w1_ref, bias_ref, w2_ref, hs, sink):
    bias = bias_ref[...]
    x = place.col + column
    col_ok = (x >= 0) & (x < place.cols)
    shifted = [jnp.concatenate([_roll(v, 1 - kx, 1) for v in images], axis=1) for kx in range(3)]
    count = max(max(b) for b in blocks) + 1
    for b in range(count + 1):
        if 8 * b + 16 > shifted[0].shape[0]:
            hs[:, 64 * b:64 * b + 64, :] = jnp.zeros((2, 64, 256), jnp.bfloat16)
            continue
        t = _dot(w1_ref[...], jnp.concatenate([v[8 * b:8 * b + 16] for v in shifted], axis=0).astype(jnp.bfloat16))
        pre = t[:64] + t[64:]
        for h in range(2):
            at = slice(128 * h, 128 * h + 128)
            if b not in blocks[h] and b - 1 not in blocks[h]:
                hs[:, 64 * b:64 * b + 64, at] = jnp.zeros((2, 64, 128), jnp.bfloat16)
                continue
            v = jnp.concatenate([
                jnp.maximum(pre[CH * k:CH * k + CH, at] + bias, 0.0) * place.keep(tops[h] - 1 + 8 * b + k, col_ok)
                for k in range(8)], axis=0)
            hs[0, 64 * b:64 * b + 64, at], hs[1, 64 * b:64 * b + 64, at] = _split(v)
        yield 100
    for b in range(count):
        t = _dot(w2_ref[...], jnp.concatenate([hs[0, 64 * b:64 * b + 80], hs[1, 64 * b:64 * b + 80]], axis=0))
        v = t[:192] + t[192:]
        for h in range(2):
            if b not in blocks[h]:
                continue
            o = [v[64 * kx:64 * kx + 64, 128 * h:128 * h + 128] for kx in range(3)]
            e = o[1] + _roll(o[0], 1, 1) + _roll(o[2], -1, 1)
            sink(b, h, [e[CH * k:CH * k + CH] * place.keep(tops[h] + 8 * b + k, col_ok) for k in range(8)])
        yield 120


def _build(moving, fixed, window, pixel, e3, ef):
    lane = lax.broadcasted_iota(jnp.int32, (8, 128), 1)
    for r in range(0, PROWS, 2):
        out = []
        for k in (r, r + 1):
            e0 = jnp.where(lane < 64, _roll(moving[k], -window, 1), _roll(moving[k + CUT], 64 - window, 1))
            left, right = _roll(e0, 1, 1), _roll(e0, -1, 1)
            p1 = 0.5 * (right - left)
            p2 = 0.5 * (right + left) - e0
            out += [e0 + 0.25 * p2, p1, p2]
        hi, lo = _split(jnp.concatenate(out, axis=0))
        e3[24 * r:24 * r + 48, 0:128] = hi
        e3[24 * r:24 * r + 48, 128:256] = lo
        yield 25
    for q in range(NQ):
        cur = None
        for i in range(4):
            row = min(max(4 * q - 4 + i, -2), TR + 1) - TOP
            v = _roll(fixed[row], 32 * i - pixel, 1)
            cur = v if i == 0 else jnp.where(lane < 32 * i, cur, v)
        ef[q] = cur
        yield 25


def _start(field, pixel, s, raw):
    lane = lax.broadcasted_iota(jnp.int32, (8, 128), 1)
    sub = lax.broadcasted_iota(jnp.int32, (8, 128), 0)
    mine = lane // 32 == sub % 4
    for comp in range(2):
        for b in range(NQ // 2):
            v = field[comp][8 * b + 4:8 * b + 12]
            v = _pick(v, (lane - 32 * (sub % 4) + pixel) & 127)
            for k in range(2):
                raw[comp, 2 * b + k, s:s + 1, :] = jnp.sum(
                    jnp.where(mine & (sub // 4 == k), v, 0.0), axis=0, keepdims=True)


def _middle(own_ref, up_ref, down_ref, w1_ref, bias_ref, w2_ref, e3_ref, ef_ref, raw_ref, rows_ref, hs):
    moving, fixed, *field = _tall(_own(own_ref), up_ref[...], down_ref[...])
    lane = lax.broadcasted_iota(jnp.int32, (CH, 128), 1)
    rows = [{}, {}]

    def sink(b, h, got):
        for k, v in enumerate(got):
            rows[h][8 * b + k] = v
            rows_ref[h, 8 * b + k] = v

    blank = jnp.zeros((16, 128), jnp.float32)
    fixed = jnp.concatenate([blank, fixed, blank], axis=0)
    for _ in _embed(_Place(), [moving, fixed], lane, [TOP, TOP], [range(BLOCKS), FIXED_BLOCKS],
                    w1_ref, bias_ref, w2_ref, hs, sink):
        pass
    raw_ref[...] = jnp.zeros_like(raw_ref)
    for s in range(1, SEGS - 1):
        _start(field, WIDE * s - SIDE, s, raw_ref)
        for _ in _build(rows[0], rows[1], WIDE * s - 3 - REACH, WIDE * s - SIDE, e3_ref.at[s - 1], ef_ref.at[s - 1]):
            pass


def _refine(own_ref, up_ref, down_ref, one_ref, two_ref, w1_ref, bias_ref, w2_ref, mid3_ref, midf_ref, midr_ref, rows_ref,
            out_ref, hs, e3, ef, raw, m1, m2, sq, disp, frac, idx, dat):
    place = _Place()
    row0, col0, rows, cols = place.row, place.col, place.rows, place.cols
    lane = lax.broadcasted_iota(jnp.int32, (8, 128), 1)
    sub = lax.broadcasted_iota(jnp.int32, (8, 128), 0)
    image, *field = _edges(_own(own_ref), up_ref[...], down_ref[...], one_ref[...], two_ref[...])
    raw[...] = midr_ref[...]
    _start(field, REACH, 0, raw)
    _start(field, AT4 + REACH, SEGS - 1, raw)
    tables = [e3.at[0]] + [mid3_ref.at[k] for k in range(SEGS - 2)] + [e3.at[1]]
    targets = [ef.at[0]] + [midf_ref.at[k] for k in range(SEGS - 2)] + [ef.at[1]]

    def edges(ready):
        rows = [[{}, {}], [{}, {}]]

        def sink(b, h, got):
            for k, v in enumerate(got):
                r = 8 * (b + HALF * h) + k
                mine = rows_ref[0, r]
                rows[0][0][r] = jnp.where(lane < FROM0 + 2, _roll(v, FROM0 - HALO_M, 1), _roll(mine, FROM0, 1))
                rows[1][0][r] = jnp.where(lane < TC - FROM4 - 2, _roll(mine, -FROM4, 1), _roll(v, FAR - 32 - FROM4, 1))
                if r // 8 in FIXED_BLOCKS:
                    mine = rows_ref[1, r]
                    rows[0][1][r] = jnp.where(lane < FROM0 + 2, _roll(v, FROM0 - HALO_M - 64, 1), _roll(mine, FROM0, 1))
                    rows[1][1][r] = jnp.where(lane < TC - FROM4 - 2, _roll(mine, -FROM4, 1), _roll(v, FAR - 96 - FROM4, 1))

        column = jnp.where(lane % 64 < 32, lane % 32 - HALO_M, lane % 32 + FAR)
        blank = jnp.zeros((8, 128), jnp.float32)
        halves = [image[:8 * HALF + 16], jnp.concatenate([image[8 * HALF:], blank, blank], axis=0)]
        yield from _embed(place, halves, column, [TOP, TOP + 8 * HALF], [range(HALF), range(BLOCKS - HALF)],
                          w1_ref, bias_ref, w2_ref, hs, sink)
        yield from _build(rows[0][0], rows[0][1], 0, REACH, e3.at[0], ef.at[0])
        ready.extend((q0, 0) for q0 in range(0, NQ, 2))
        yield from _build(rows[1][0], rows[1][1], AT4, AT4 + REACH, e3.at[1], ef.at[1])
        ready.extend((q0, SEGS - 1) for q0 in range(0, NQ, 2))

    dat[...] = jnp.zeros_like(dat)

    j = lane % 32
    x = col0 + WIDE * sub - SIDE + j
    col_in = (x >= 0) & (x < cols)
    iota_k = lax.broadcasted_iota(jnp.int32, (128, 256), 0).astype(jnp.float32).astype(jnp.bfloat16)

    def group(q0, s):
        start = max(4 * q0 - 4, -2) + 2

        def pair(ref, comp, count):
            return jnp.concatenate(
                [jnp.broadcast_to(ref[comp, q0 + k, s:s + 1, :], (count, 128)) for k in range(2)], axis=1)

        col = pair(idx, 1, 1) + jnp.where(pair(idx, 0, 1) >= start + CUT, 64.0, 0.0)
        pick = jnp.where(iota_k == jnp.broadcast_to(col.astype(jnp.bfloat16), (128, 256)),
                         jnp.bfloat16(1.0), jnp.bfloat16(0.0))
        count = CUT + 2
        t = _dot(tables[s][24 * start:24 * (start + count), :], jnp.concatenate([pick, pick], axis=0))
        base = pair(idx, 0, 8) - (start * 1.0)
        base = jnp.where(base >= CUT, base - CUT, base)
        conds = []
        for cut in _levels(CUT):
            c = base >= cut
            conds.append((cut, c))
            base = jnp.where(c, base - cut, base)
        taps = []
        for b in range(3):
            T = [t[24 * k + 8 * b:24 * k + 8 * b + 8] for k in range(count)]
            for cut, c in conds:
                T = [jnp.where(c, T[k + cut], T[k]) if k + cut < len(T) else T[k] for k in range(cut + 2)]
            taps.append(T)
        fr, fc = pair(frac, 0, 8), pair(frac, 1, 8)
        A, B = [], []
        for a in range(3):
            w = fc * taps[2][a]
            v = taps[1][a] + w
            A.append(taps[0][a] + fc * v)
            B.append(v + w)
        da, qa = 0.5 * (A[2] - A[0]), 0.5 * (A[2] + A[0]) - A[1]
        db, qb = 0.5 * (B[2] - B[0]), 0.5 * (B[2] + B[0]) - B[1]
        wa = fr * qa
        va = da + wa
        warped = A[1] + 0.25 * qa + fr * va
        slope_row = va + wa
        slope_col = B[1] + 0.25 * qb + fr * (db + fr * qb)
        target = jnp.concatenate([targets[s][q0], targets[s][q0 + 1]], axis=1)
        miss = (warped - target) * (2.0 / CH)
        for comp, slope in ((0, slope_row), (1, slope_col)):
            total = jnp.sum(miss * slope, axis=0, keepdims=True)
            for k in range(2):
                dat[comp, q0 + k, s:s + 1, :] = total[:, 128 * k:128 * k + 128]

    def step(t):
        for q in range(NQ):
            y = 4 * q - 4 + lane // 32
            ok = col_in & (row0 + y >= 0) & (row0 + y < rows)
            for comp, origin in ((0, y + REACH + 2), (1, j + REACH)):
                v = jnp.tanh(raw[comp, q] * (1.0 / REACH))
                d = REACH * v
                n = jnp.floor(d + 0.5)
                sq[comp, q] = v
                disp[comp, q] = jnp.where(ok, d, 0.0)
                frac[comp, q] = d - n
                idx[comp, q] = n + origin.astype(jnp.float32)
        if t == 0:
            ready, spent = [(q0, s) for s in range(1, SEGS - 1) for q0 in range(0, NQ, 2)], 0
            for length in edges(ready):
                spent += length
                while spent >= PACE and ready:
                    spent -= PACE
                    group(*ready.pop(0))
            for at in ready:
                group(*at)
        for q0 in range(0, NQ, 2) if t < 2 else range(1, NQ - 1, 2):
            if t > 0:
                for s in range(SEGS):
                    group(q0, s)
            for comp in range(2):
                for q in (q0, q0 + 1):
                    update(t, comp, q)
                if t == 2:
                    finish(comp, q0 // 2)

    def update(t, comp, q):
        one, two = 1.0 / (1.0 - 0.9 ** (t + 1)), 1.0 / (1.0 - 0.999 ** (t + 1))
        d = disp[comp, q]
        up = jnp.where(lane < 96, _roll(d, -32, 1), _roll(disp[comp, min(q + 1, NQ - 1)], -32, 1))
        down = jnp.where(lane >= 32, _roll(d, 32, 1), _roll(disp[comp, max(q - 1, 0)], 32, 1))
        around = up + down + _roll(d, 1, 1) + _roll(d, -1, 1)
        v = sq[comp, q]
        grad = (dat[comp, q] + 2.0 * STIFFNESS * (4.0 * REACH * v - around)) * (1.0 - v * v)
        a, b = 0.1 * grad, 0.001 * grad * grad
        if t > 0:
            a, b = 0.9 * m1[comp, q] + a, 0.999 * m2[comp, q] + b
        m1[comp, q] = a
        m2[comp, q] = b
        raw[comp, q] = raw[comp, q] - STEP * (a * one) / (jnp.sqrt(b * two) + EPS)

    own = _own(own_ref)

    def finish(comp, b):
        out = None
        for s in range(SEGS):
            v = jnp.where(sub < 4, jnp.broadcast_to(raw[comp, 2 * b + 1, s:s + 1, :], (8, 128)),
                          jnp.broadcast_to(raw[comp, 2 * b + 2, s:s + 1, :], (8, 128)))
            v = _pick(v, (lane + 32 * (sub % 4) + (128 + SIDE - WIDE * s)) & 127)
            out = v if s == 0 else jnp.where(lane < WIDE * s, out, v)
        out_ref[comp, 8 * b:8 * b + 8] = out - own[2 + comp][8 * b:8 * b + 8]

    for t in range(ITERS):
        step(t)


def _swaps(axis, first):
    rows, cols = lax.axis_size("row"), lax.axis_size("col")
    n = rows if axis == "row" else cols
    out = []
    for r in range(rows):
        for c in range(cols):
            i = r if axis == "row" else c
            j = i + 1 if (i - first) % 2 == 0 else i - 1
            if 0 <= j < n:
                r2, c2 = (j, c) if axis == "row" else (r, j)
            elif axis == "row":
                r2, c2 = r, c ^ 1
            else:
                r2, c2 = r ^ 1, c
            out.append((r * cols + c, r2 * cols + c2))
    return out


def _exchange(pair, axis):
    return [lax.ppermute(x, ("row", "col"), _swaps(axis, k)) for k, x in enumerate(pair)]


def _local(fixed_section, moving_section, field_init, first_weight, first_bias, second_weight):
    vmem = pl.BlockSpec(memory_space=pltpu.VMEM)
    smem = pl.BlockSpec(memory_space=pltpu.SMEM)
    anywhere = pl.BlockSpec(memory_space=pltpu.HBM)
    f32, bf16 = jnp.float32, jnp.bfloat16

    def call(body, name, out, specs, scratch):
        return pl.pallas_call(
            body,
            out_shape=[jax.ShapeDtypeStruct(*x) for x in out],
            in_specs=specs,
            out_specs=[vmem] * len(out),
            scratch_shapes=scratch,
            compiler_params=pltpu.CompilerParams(vmem_limit_bytes=48 * 2 ** 20),
            name=name,
        )

    strip = ((sum(PADS), 128), f32)
    one, two, own = call(_pack_rows, "pack_rows", [strip, strip, ((4 * TR, TC), f32)], [anywhere] * 3, [
        pltpu.VMEM((TR, TC), bf16), pltpu.VMEM((TR, TC), bf16), pltpu.VMEM((2, TR, TC), f32),
        pltpu.SemaphoreType.DMA((3,))])(*[pltpu.with_memory_space_constraint(x, pltpu.HBM) for x in (moving_section, fixed_section, field_init)])
    up, down = _exchange((one, two), "row")
    w1, w2, bias = call(_weights, "weights", [((128, 48), bf16), ((384, 160), bf16), ((CH, 128), f32)],
                        [anywhere, anywhere, smem], [
        pltpu.VMEM((CH, 9), f32), pltpu.VMEM((CH, CH, 9), f32), pltpu.VMEM((2, CH, 128), f32),
        pltpu.SemaphoreType.DMA((2,))])(*[pltpu.with_memory_space_constraint(x, pltpu.HBM) for x in (first_weight, second_weight)], first_bias)
    strip = ((8 * pl.cdiv(TALL, 32), 128), f32)
    one, two = _exchange(call(_pack_cols, "pack_cols", [strip, strip], [vmem] * 4, [])(own, up, down, bias), "col")
    hidden = pltpu.VMEM((2, HROWS * CH, 256), bf16)
    table, target = (PROWS * 24, 256), (NQ, CH, 128)
    mid = call(_middle, "middle", [
        ((SEGS - 2,) + table, bf16), ((SEGS - 2,) + target, f32), ((2, NQ, 8, 128), f32), ((2, EROWS, CH, 128), f32),
    ], [vmem] * 6, [hidden])(own, up, down, w1, bias, w2)
    return call(_refine, "refine", [((2, TR, TC), f32)], [vmem] * 12, [
        hidden, pltpu.VMEM((2,) + table, bf16), pltpu.VMEM((2,) + target, f32),
        *[pltpu.VMEM((2, NQ, 8, 128), f32) for _ in range(8)],
    ])(own, up, down, one, two, w1, bias, w2, *mid)[0]


def solution(mesh):
    return jax.shard_map(
        _local,
        mesh=mesh,
        in_specs=(P("row", "col"), P("row", "col"), P(None, "row", "col"), P(), P(), P()),
        out_specs=P(None, "row", "col"),
        check_vma=False,
    )
```
